256 devices in a mesh: seq: 32 (over z, y), ch: 8 (over x, core).
Axes of the slice: x: 4, y: 4, z: 8, core: 2. Of those that a mesh axis runs over, the one named last changes fastest.
Arguments:
- signal: float32 [32768, 1536], P('seq', 'ch'), may hold values from -6 to 6
- cotangent: float32 [32768, 1536], P('seq', 'ch'), may hold values from -6 to 6
- kernel_q: float32 [3, 1536], P(None, 'ch'), may hold values from -3 to 3
- kernel_k: float32 [3, 1536], P(None, 'ch'), may hold values from -3 to 3
- block_first: float32 [32, 1024, 1024], P('seq'), may hold values from -0.1875 to 0.1875
- block_second: float32 [32, 1024, 1024], P('seq'), may hold values from -0.1875 to 0.1875
- mix_self: float32 [5, 32, 1536], P(None, 'seq', 'ch'), may hold values from 0.5 to 1
- mix_partner: float32 [5, 32, 1536], P(None, 'seq', 'ch'), may hold values from -1 to 1
Outputs:
- output: float32 [32768, 1536], P('seq', 'ch')
- grad_signal: float32 [32768, 1536], P('seq', 'ch')
- grad_kernel_q: float32 [3, 1536], P(None, 'ch')
- grad_kernel_k: float32 [3, 1536], P(None, 'ch')
- grad_block_first: float32 [32, 1024, 1024], P('seq', 'ch')
- grad_block_second: float32 [32, 1024, 1024], P('seq', 'ch')
- grad_mix_self: float32 [5, 32, 1536], P(None, 'seq', 'ch')
- grad_mix_partner: float32 [5, 32, 1536], P(None, 'seq', 'ch')
The draws below stay inside these ranges and needn't reach their ends.
All inputs are finite; a program needn't handle non-finite values.
Results may differ from the reference program's by a relative error of at most 0.00015.
Values sent between devices are 32-bit elements; how exact they have to be, the bound alone decides.
No kernel may reach another device: no remote copies, remote signals or barrier semaphores. Data moves between devices by JAX's collectives and lax.ppermute only.
A program may use at most 128 MiB of HBM per device.

```python
import math
import jax
import jax.numpy as jnp
from jax import lax

D = 1536
ROWS = 1024
TAPS = 3
LOGS = 5
TOKENS = 32768
N_SEQ = 32


def block_levels(stream_key, extent, split, low, high):
    level, own = 1.0, jax.random.fold_in(stream_key, 6)
    for axis_at, shards_of in split:
        steps = jnp.exp(jax.random.uniform(jax.random.fold_in(own, axis_at), (shards_of,), jnp.float32, low / len(split), high / len(split)))
        level = level * jnp.repeat(steps, extent[axis_at] // shards_of).reshape([-1 if axis == axis_at else 1 for axis in range(len(extent))])
    return level


def noise(rng, dims, spread, bound, pieces=(), dtype=jnp.bfloat16):
    entries = spread * jax.random.normal(rng, dims, jnp.float32)
    if pieces:
        entries = entries * block_levels(rng, dims, pieces, -0.22, 0.18)
    return jnp.clip(entries, -bound, bound).astype(dtype)


def setup_inputs(seed: int = 0) -> dict:
    key_of = jax.random.split(jax.random.key(seed), 9)
    signal = noise(key_of[0], (TOKENS, D), 1.0, 6.0, ((0, 32), (1, 8)), jnp.float32)
    cotangent = noise(key_of[1], (TOKENS, D), 1.0, 6.0, ((0, 32), (1, 8)), jnp.float32)
    kernel_q = noise(key_of[2], (TAPS, D), 0.6, 3.0, ((1, 8),), jnp.float32)
    kernel_k = noise(key_of[3], (TAPS, D), 0.6, 3.0, ((1, 8),), jnp.float32)
    block_first = noise(key_of[4], (N_SEQ, ROWS, ROWS), ROWS ** -0.5, 0.1875, ((0, 32),), jnp.float32)
    block_second = noise(key_of[5], (N_SEQ, ROWS, ROWS), ROWS ** -0.5, 0.1875, ((0, 32),), jnp.float32)
    mix_self = jnp.clip(0.5 + 0.5 * jax.random.uniform(key_of[6], (LOGS, N_SEQ, D), jnp.float32) ** block_levels(key_of[6], (LOGS, N_SEQ, D), ((1, 32), (2, 8)), -0.2, 0.2), 0.5, 1.0)
    mix_partner = jnp.clip(jax.random.uniform(key_of[7], (LOGS, N_SEQ, D), jnp.float32, -1.0, 1.0) * block_levels(key_of[7], (LOGS, N_SEQ, D), ((1, 32), (2, 8)), -0.4, 0.0), -1.0, 1.0)
    return {"signal": signal, "cotangent": cotangent, "kernel_q": kernel_q, "kernel_k": kernel_k, "block_first": block_first, "block_second": block_second, "mix_self": mix_self, "mix_partner": mix_partner}


exact_mode = lax.Precision.HIGHEST

def short_conv(values, taps_table):
    padded = jnp.pad(values, ((1, 1), (0, 0)))
    return taps_table[0] * padded[:-2] + taps_table[1] * padded[1:-1] + taps_table[2] * padded[2:]

def flip_partner(current, section_bit):
    blocks = current.shape[0]
    stride = 2 ** section_bit
    grouped = current.reshape((blocks // (2 * stride), 2, stride) + current.shape[1:])
    return jnp.flip(grouped, 1).reshape(current.shape)

def forward(signal, kernel_q, kernel_k, block_first, block_second, mix_self, mix_partner):
    query_conv = short_conv(signal, kernel_q)
    key_conv = short_conv(signal, kernel_k)
    blocks = block_first.shape[0]
    gated_in = (key_conv * signal).reshape(blocks, -1, signal.shape[1])
    current = jnp.einsum('prs,psd->prd', block_first, gated_in, precision=exact_mode)
    for section_bit in range(mix_self.shape[0]):
        partner = flip_partner(current, section_bit)
        current = mix_self[section_bit][:, None, :] * current + mix_partner[section_bit][:, None, :] * partner
    mixed_out = jnp.einsum('prs,psd->prd', block_second, current, precision=exact_mode)
    return query_conv * mixed_out.reshape(signal.shape)

def reference(signal, cotangent, kernel_q, kernel_k, block_first, block_second, mix_self, mix_partner):
    output, pullback = jax.vjp(forward, signal, kernel_q, kernel_k, block_first, block_second, mix_self, mix_partner)
    grads = pullback(cotangent)
    tok_scale = 1.0 / math.sqrt(TOKENS)
    width_scale = 1.0 / math.sqrt(D)
    row_scale = 1.0 / math.sqrt(ROWS)
    return (output, grads[0], grads[1] * tok_scale, grads[2] * tok_scale, grads[3] * width_scale, grads[4] * width_scale, grads[5] * row_scale, grads[6] * row_scale)
```

```python
import math

import jax
import jax.numpy as jnp
from jax import lax
from jax.experimental import pallas as pl
from jax.experimental.pallas import tpu as pltpu
from jax.sharding import PartitionSpec as P

D = 1536
SECTIONS = 5
BLOCKS = 32
PARTS = ((0, 4), (4, 6))
LANE_OF_PART = (0, 64)

three_pass = lax.Precision.HIGH


def contract(left, right, left_dim, right_dim):
    return lax.dot_general(
        left,
        right,
        (((left_dim,), (right_dim,)), ((), ())),
        precision=three_pass,
        preferred_element_type=jnp.float32,
    )


def to_tiles(values):
    first = values[:128].reshape(16, 8, 2, 4, 128).transpose(0, 2, 3, 1, 4).reshape(32, 4, 8, 128)
    second = values[128:].reshape(8, 8, 4, 2, 128).transpose(0, 2, 3, 1, 4).reshape(32, 2, 8, 128)
    return jnp.concatenate([first, second], axis=1)


def from_tiles(tiles):
    first = tiles[:, :4].reshape(16, 2, 4, 8, 128).transpose(0, 3, 1, 2, 4).reshape(128, 1024)
    second = tiles[:, 4:].reshape(8, 4, 2, 8, 128).transpose(0, 3, 1, 2, 4).reshape(64, 1024)
    return jnp.concatenate([first, second], axis=0)


def weights_to_tile(weights):
    first = jnp.repeat(weights[:128].reshape(16, 8, 2 * SECTIONS), 2, axis=0)
    second = jnp.repeat(weights[128:].reshape(8, 8, 2 * SECTIONS), 4, axis=0)
    gap = ((0, 0), (0, 0), (0, 64 - 2 * SECTIONS))
    return jnp.concatenate([jnp.pad(first, gap), jnp.pad(second, gap)], axis=2)[:, None]


def tile_to_weights(tile):
    first = tile[:, :, : 2 * SECTIONS].reshape(16, 2, 8, 2 * SECTIONS).sum(axis=1)
    second = tile[:, :, 64 : 64 + 2 * SECTIONS].reshape(8, 4, 8, 2 * SECTIONS).sum(axis=1)
    return jnp.concatenate([first.reshape(128, 2 * SECTIONS), second.reshape(64, 2 * SECTIONS)], axis=0)


def flip(values, section):
    stride = 2**section
    pieces = []
    for at in range(0, BLOCKS, 2 * stride):
        pieces.append(values[at + stride : at + 2 * stride])
        pieces.append(values[at : at + stride])
    return jnp.concatenate(pieces, axis=0)


def butterfly_kernel(in_ref, out_ref, weight_ref, level_ref, sum_ref):
    for part, (low, high) in enumerate(PARTS):
        lane = LANE_OF_PART[part]
        for at in range(2 * SECTIONS):
            column = in_ref[:, 12, :, lane + at : lane + at + 1]
            weight_ref[part, at] = jnp.broadcast_to(column, (BLOCKS, 8, 128))

        def one_tile(tile, first):
            level = in_ref[:, tile]
            for section in range(SECTIONS):
                level_ref[section] = level
                level = (
                    weight_ref[part, section] * level
                    + weight_ref[part, SECTIONS + section] * flip(level, section)
                )
            out_ref[:, tile] = level
            grad = in_ref[:, 6 + tile]
            for section in reversed(range(SECTIONS)):
                level = level_ref[section]
                own = grad * level
                other = grad * flip(level, section)
                if first:
                    sum_ref[part, section] = own
                    sum_ref[part, SECTIONS + section] = other
                else:
                    sum_ref[part, section] += own
                    sum_ref[part, SECTIONS + section] += other
                grad = weight_ref[part, section] * grad + flip(
                    weight_ref[part, SECTIONS + section] * grad, section
                )
            out_ref[:, 6 + tile] = grad

        one_tile(low, True)

        def body(tile, carry):
            one_tile(tile, False)
            return carry

        lax.fori_loop(low + 1, high, body, 0)

    lanes = lax.broadcasted_iota(jnp.int32, (BLOCKS, 8, 128), 2)
    result = jnp.zeros((BLOCKS, 8, 128), jnp.float32)
    for part in range(2):
        for at in range(2 * SECTIONS):
            total = jnp.sum(sum_ref[part, at], axis=2, keepdims=True)
            result = jnp.where(lanes == LANE_OF_PART[part] + at, total, result)
    out_ref[:, 12] = result


def butterfly(tiles):
    return pl.pallas_call(
        butterfly_kernel,
        out_shape=jax.ShapeDtypeStruct(tiles.shape, jnp.float32),
        in_specs=[pl.BlockSpec(memory_space=pltpu.VMEM)],
        out_specs=pl.BlockSpec(memory_space=pltpu.VMEM),
        scratch_shapes=[
            pltpu.VMEM((2, 2 * SECTIONS, BLOCKS, 8, 128), jnp.float32),
            pltpu.VMEM((SECTIONS, BLOCKS, 8, 128), jnp.float32),
            pltpu.VMEM((2, 2 * SECTIONS, BLOCKS, 8, 128), jnp.float32),
        ],
        compiler_params=pltpu.CompilerParams(vmem_limit_bytes=32 * 1024 * 1024),
        cost_estimate=pl.CostEstimate(flops=16_000_000, bytes_accessed=3_500_000, transcendentals=0),
        name="butterfly",
    )(tiles)


def neighbours(low_column, high_column):
    count = lax.axis_size("seq")
    before = lax.ppermute(low_column, "seq", [(i, i + 1) for i in range(count - 1)])
    after = lax.ppermute(high_column, "seq", [(i + 1, i) for i in range(count - 1)])
    return before, after


def local(signal, cotangent, kernel_q, kernel_k, block_first, block_second, mix_self, mix_partner):
    height, breadth = signal.shape
    blocks = lax.axis_size("seq")
    signal, cotangent = signal.T, cotangent.T
    taps_q, taps_k = kernel_q.T, kernel_k.T
    first, second = block_first[0], block_second[0]

    before, after = neighbours(signal[:, -1:], signal[:, :1])
    padded = jnp.concatenate([before, signal, after], axis=1)

    def conv(taps):
        return taps[:, 0:1] * padded[:, :-2] + taps[:, 1:2] * signal + taps[:, 2:3] * padded[:, 2:]

    query_conv = conv(taps_q)
    key_conv = conv(taps_k)
    gated_in = key_conv * signal
    grad_mixed = cotangent * query_conv
    first_out = contract(gated_in, first, 1, 1)
    grad_last = contract(grad_mixed, second, 1, 0)

    weights = jnp.concatenate([mix_self[:, 0], mix_partner[:, 0]], axis=0).T
    outgoing = jnp.concatenate([to_tiles(first_out), to_tiles(grad_last), weights_to_tile(weights)], axis=1)
    incoming = lax.all_to_all(outgoing, "seq", 0, 0, tiled=True)
    mixed = butterfly(incoming)
    returned = lax.all_to_all(mixed, "seq", 0, 0, tiled=True)
    level_last = from_tiles(returned[:, :6])
    grad_first_level = from_tiles(returned[:, 6:12])
    mix_grads = tile_to_weights(returned[:, 12]).T * (1.0 / math.sqrt(height))

    grad_blocks = jnp.stack(
        [contract(grad_first_level, gated_in, 0, 0), contract(grad_mixed, level_last, 0, 0)]
    )
    summed = lax.psum_scatter(grad_blocks, "ch", scatter_dimension=1, tiled=True) * (1.0 / math.sqrt(D))

    grad_gated = contract(grad_first_level, first, 1, 0)
    grad_key = grad_gated * signal
    mixed_out = contract(level_last, second, 1, 1)
    output = query_conv * mixed_out
    grad_query = cotangent * mixed_out

    edges = jnp.stack([grad_query, grad_key])
    edge_before, edge_after = neighbours(edges[:, :, -1:], edges[:, :, :1])
    edge_pad = jnp.concatenate([edge_before, edges, edge_after], axis=2)
    grad_signal = grad_gated * key_conv
    for at, taps in enumerate((taps_q, taps_k)):
        grad_signal = (
            grad_signal
            + taps[:, 0:1] * edge_pad[at, :, 2:]
            + taps[:, 1:2] * edges[at]
            + taps[:, 2:3] * edge_pad[at, :, :-2]
        )

    sums = jnp.stack(
        [
            jnp.sum(rows * shifted, axis=1)
            for rows in (grad_query, grad_key)
            for shifted in (padded[:, :-2], signal, padded[:, 2:])
        ]
    )
    sums = jnp.pad(sums.reshape(-1), (0, 16 * 128 - sums.size)).reshape(1, 16, 128)
    everyone = lax.all_to_all(jnp.broadcast_to(sums, (blocks, 16, 128)), "seq", 0, 0, tiled=True)
    tap_total = jnp.sum(everyone, axis=0).reshape(-1)[: 6 * breadth].reshape(2, 3, breadth)
    tap_total = tap_total * (1.0 / math.sqrt(height * blocks))

    return (
        output.T,
        grad_signal.T,
        tap_total[0],
        tap_total[1],
        summed[0][None],
        summed[1][None],
        mix_grads[:SECTIONS, None],
        mix_grads[SECTIONS:, None],
    )


def solution(mesh):
    return jax.shard_map(
        local,
        mesh=mesh,
        in_specs=(
            P("seq", "ch"),
            P("seq", "ch"),
            P(None, "ch"),
            P(None, "ch"),
            P("seq", None, None),
            P("seq", None, None),
            P(None, "seq", "ch"),
            P(None, "seq", "ch"),
        ),
        out_specs=(
            P("seq", "ch"),
            P("seq", "ch"),
            P(None, "ch"),
            P(None, "ch"),
            P("seq", "ch", None),
            P("seq", "ch", None),
            P(None, "seq", "ch"),
            P(None, "seq", "ch"),
        ),
        check_vma=False,
    )
```

```python
import math

import jax
import jax.numpy as jnp
from jax import lax
from jax.experimental import pallas as pl
from jax.experimental.pallas import tpu as pltpu
from jax.sharding import PartitionSpec as P

D = 1536
SECTIONS = 5
BLOCKS = 32
PARTS = ((0, 4), (4, 6))
LANE_OF_PART = (0, 64)
WEIGHT_TILE = 6
CHIPS = 4
STEPS = (2, 1, 3, 0)
COLUMNS = 256
VMEM_LIMIT = 56 * 1024 * 1024
WIDTH_SCALE = 1.0 / math.sqrt(D)
ROW_SCALE = 1.0 / math.sqrt(1024)
TOKEN_SCALE = 1.0 / math.sqrt(32768)

def flip(values, section):
    stride = 2**section
    pieces = []
    for at in range(0, BLOCKS, 2 * stride):
        pieces.append(values[at + stride : at + 2 * stride])
        pieces.append(values[at : at + stride])
    return jnp.concatenate(pieces, axis=0)


def load_weights(in_ref, weight_ref):
    for part in range(2):
        for at in range(2 * SECTIONS):
            lane = LANE_OF_PART[part] + at
            column = in_ref[:, 12, :, lane : lane + 1]
            weight_ref[part, at] = jnp.broadcast_to(column, (BLOCKS, 8, 128))


def step_forward(level, weight_ref, part, section):
    return (
        weight_ref[part, section] * level
        + weight_ref[part, SECTIONS + section] * flip(level, section)
    )


def forward_kernel(in_ref, out_ref, weight_ref):
    load_weights(in_ref, weight_ref)
    for part, (low, high) in enumerate(PARTS):

        def one_tile(tile, carry):
            level = in_ref[:, tile]
            for section in range(SECTIONS):
                level = step_forward(level, weight_ref, part, section)
            out_ref[:, tile] = level
            return carry

        lax.fori_loop(low, high, one_tile, 0)


def backward_kernel(in_ref, out_ref, weight_ref, level_ref, sum_ref):
    load_weights(in_ref, weight_ref)
    for part, (low, high) in enumerate(PARTS):

        def one_tile(tile, first):
            level = in_ref[:, tile]
            for section in range(SECTIONS):
                level_ref[section] = level
                if section < SECTIONS - 1:
                    level = step_forward(level, weight_ref, part, section)
            grad = in_ref[:, 6 + tile]
            for section in reversed(range(SECTIONS)):
                level = level_ref[section]
                own = grad * level
                other = grad * flip(level, section)
                if first:
                    sum_ref[part, section] = own
                    sum_ref[part, SECTIONS + section] = other
                else:
                    sum_ref[part, section] += own
                    sum_ref[part, SECTIONS + section] += other
                grad = weight_ref[part, section] * grad + flip(
                    weight_ref[part, SECTIONS + section] * grad, section
                )
            out_ref[:, tile] = grad

        one_tile(low, True)

        def body(tile, carry):
            one_tile(tile, False)
            return carry

        lax.fori_loop(low + 1, high, body, 0)

    lanes = lax.broadcasted_iota(jnp.int32, (BLOCKS, 8, 128), 2)
    result = jnp.zeros((BLOCKS, 8, 128), jnp.float32)
    for part in range(2):
        for at in range(2 * SECTIONS):
            total = jnp.sum(sum_ref[part, at], axis=2, keepdims=True)
            result = jnp.where(lanes == LANE_OF_PART[part] + at, total, result)
    out_ref[:, WEIGHT_TILE] = result


WEIGHT_SCRATCH = (2, 2 * SECTIONS, BLOCKS, 8, 128)
IN_VMEM = pl.BlockSpec(memory_space=pltpu.VMEM)


def butterfly_forward(tiles):
    return pl.pallas_call(
        forward_kernel,
        out_shape=jax.ShapeDtypeStruct((BLOCKS, 6, 8, 128), jnp.float32),
        in_specs=[IN_VMEM],
        out_specs=IN_VMEM,
        scratch_shapes=[pltpu.VMEM(WEIGHT_SCRATCH, jnp.float32)],
        compiler_params=pltpu.CompilerParams(vmem_limit_bytes=24 * 1024 * 1024),
        cost_estimate=pl.CostEstimate(flops=4_000_000, bytes_accessed=1_800_000, transcendentals=0),
        name="butterfly_forward",
    )(tiles)


def butterfly_backward(tiles):
    return pl.pallas_call(
        backward_kernel,
        out_shape=jax.ShapeDtypeStruct((BLOCKS, 7, 8, 128), jnp.float32),
        in_specs=[IN_VMEM],
        out_specs=IN_VMEM,
        scratch_shapes=[
            pltpu.VMEM(WEIGHT_SCRATCH, jnp.float32),
            pltpu.VMEM((SECTIONS, BLOCKS, 8, 128), jnp.float32),
            pltpu.VMEM(WEIGHT_SCRATCH, jnp.float32),
        ],
        compiler_params=pltpu.CompilerParams(vmem_limit_bytes=32 * 1024 * 1024),
        cost_estimate=pl.CostEstimate(flops=12_000_000, bytes_accessed=2_600_000, transcendentals=0),
        name="butterfly_backward",
    )(tiles)


def neighbours(low, high):
    count = lax.axis_size("seq")
    before = lax.ppermute(low, "seq", [(i, i + 1) for i in range(count - 1)])
    after = lax.ppermute(high, "seq", [(i + 1, i) for i in range(count - 1)])
    return before, after


def owner_and_tile(group, chunk):
    if group < 16:
        return 2 * group + chunk // 4, chunk % 4
    return 4 * (group - 16) + chunk // 2, 4 + chunk % 2


def split_two(values):
    high = values.astype(jnp.bfloat16)
    return high, (values - high.astype(jnp.float32)).astype(jnp.bfloat16)


def dot_three(left, right, left_dim, right_dim):
    def dot(a, b):
        return lax.dot_general(
            a, b, (((left_dim,), (right_dim,)), ((), ())), preferred_element_type=jnp.float32
        )

    (left_high, left_low), (right_high, right_low) = left, right
    return dot(left_high, right_high) + (dot(left_high, right_low) + dot(left_low, right_high))


def unpack(tile_ref, dest_ref, row):
    for group in range(24):
        for chunk in range(8):
            owner, tile = owner_and_tile(group, chunk)
            dest_ref[row + 8 * group : row + 8 * group + 8, 128 * chunk : 128 * chunk + 128] = (
                tile_ref[owner, tile]
            )


def chunk_of_step(place_ref, step):
    place = place_ref[0]
    return 2 * ((place // 2 + step) % CHIPS) + place % 2


def second_kernel(place_ref, left_a, left_b, right_a, right_b, *refs):
    outs, (right_ref,) = refs[:CHIPS], refs[CHIPS:]
    unpack(right_a, right_ref, 0)
    unpack(right_b, right_ref, 192)
    right = split_two(right_ref[...])
    for step in STEPS:
        rows = pl.ds(pl.multiple_of(chunk_of_step(place_ref, step) * 128, 128), 128)
        left = jnp.concatenate([left_a[:, rows], left_b[:, rows]], axis=0) * WIDTH_SCALE
        outs[step][...] = dot_three(split_two(left), right, 0, 0)


def first_kernel(place_ref, left_a, left_b, right_a, right_b, *refs):
    outs, (left_ref,) = refs[:CHIPS], refs[CHIPS:]
    right = split_two(jnp.concatenate([right_a[...], right_b[...]], axis=0))
    for step in STEPS:
        chunk = chunk_of_step(place_ref, step)
        for half, tile_ref in enumerate((left_a, left_b)):
            for group in range(24):
                owner, tile = owner_and_tile(group, chunk)
                row = 192 * half + 8 * group
                left_ref[row : row + 8, :] = tile_ref[owner, tile]
        outs[step][...] = dot_three(split_two(left_ref[...] * WIDTH_SCALE), right, 0, 0)


def prologue_kernel(
    signal_ref, cot_ref, before_ref, after_ref, column_ref, first_ref, second_ref,
    packed_ref, gated_ref, mixed_ref, query_ref, key_ref, halo_ref,
    gated_high, gated_low, mixed_high, mixed_low,
):
    at = pl.program_id(0)

    @pl.when(at == 0)
    def _():
        values = signal_ref[...]
        width = values.shape[1]
        lanes = lax.broadcasted_iota(jnp.int32, values.shape, 1)
        before = jnp.broadcast_to(before_ref[...], (128, values.shape[0])).T
        after = jnp.broadcast_to(after_ref[...], (128, values.shape[0])).T
        narrow = lax.broadcasted_iota(jnp.int32, before.shape, 1)
        halo_ref[...] = jnp.where(narrow == 0, before, after)
        prev = jnp.where(lanes == 0, before[:, :1], pltpu.roll(values, 1, 1))
        later = jnp.where(lanes == width - 1, after[:, :1], pltpu.roll(values, width - 1, 1))

        def conv(tap):
            return (
                column_ref[:, tap : tap + 1] * prev
                + column_ref[:, tap + 1 : tap + 2] * values
                + column_ref[:, tap + 2 : tap + 3] * later
            )

        query = conv(0)
        query_ref[...] = query
        key = conv(3)
        key_ref[...] = key
        gated = key * values
        gated_ref[...] = gated
        gated_high[...], gated_low[...] = split_two(gated)
        mixed = cot_ref[...] * query
        mixed_ref[...] = mixed
        mixed_high[...], mixed_low[...] = split_two(mixed)
        weights = jnp.concatenate(
            [column_ref[:, 6:16], jnp.zeros((values.shape[0], 118), jnp.float32)], axis=1
        )
        moved = pltpu.roll(weights[128:192], 64, 1)
        for owner in range(BLOCKS):
            low, high = 8 * (owner // 2), 8 * (owner // 4)
            packed_ref[owner, 12] = weights[low : low + 8] + moved[high : high + 8]

    level = dot_three((gated_high[...], gated_low[...]), split_two(first_ref[0]), 1, 1)
    grad = dot_three((mixed_high[...], mixed_low[...]), split_two(second_ref[0]), 1, 0)
    for part in range(COLUMNS // 128):
        chunk = at * (COLUMNS // 128) + part
        for group in range(24):
            owner, tile = owner_and_tile(group, chunk)
            rows, lanes = slice(8 * group, 8 * group + 8), slice(128 * part, 128 * part + 128)
            packed_ref[owner, tile] = level[rows, lanes]
            packed_ref[owner, 6 + tile] = grad[rows, lanes]


def prologue(signal, cotangent, before, after, columns, first, second):
    breadth, height = signal.shape
    whole = lambda shape: pl.BlockSpec(shape, lambda i: (0,) * len(shape))
    full = jax.ShapeDtypeStruct(signal.shape, jnp.float32)
    packed = (BLOCKS, 13, 8, 128)
    return pl.pallas_call(
        prologue_kernel,
        grid=(height // COLUMNS,),
        out_shape=[jax.ShapeDtypeStruct(packed, jnp.float32)]
        + [full] * 4
        + [jax.ShapeDtypeStruct((breadth, 128), jnp.float32)],
        in_specs=[
            whole(signal.shape),
            whole(signal.shape),
            whole(before.shape),
            whole(after.shape),
            whole(columns.shape),
            pl.BlockSpec((1, COLUMNS, height), lambda i: (0, i, 0)),
            pl.BlockSpec((1, height, COLUMNS), lambda i: (0, 0, i)),
        ],
        out_specs=[whole(packed)] + [whole(signal.shape)] * 4 + [whole((breadth, 128))],
        scratch_shapes=[pltpu.VMEM(signal.shape, jnp.bfloat16)] * 4,
        compiler_params=pltpu.CompilerParams(vmem_limit_bytes=VMEM_LIMIT),
        cost_estimate=pl.CostEstimate(flops=2_400_000_000, bytes_accessed=15_000_000, transcendentals=0),
        name="prologue",
    )(signal, cotangent, before, after, columns, first, second)


def block_products(kernel, scratch, name, place, *operands):
    piece = jax.ShapeDtypeStruct((128, 1024), jnp.float32)
    return pl.pallas_call(
        kernel,
        out_shape=[piece] * CHIPS,
        in_specs=[pl.BlockSpec(memory_space=pltpu.SMEM)] + [pl.BlockSpec()] * 4,
        out_specs=[pl.BlockSpec()] * CHIPS,
        scratch_shapes=[pltpu.VMEM(scratch, jnp.float32)],
        compiler_params=pltpu.CompilerParams(vmem_limit_bytes=VMEM_LIMIT),
        cost_estimate=pl.CostEstimate(flops=1_200_000_000, bytes_accessed=5_000_000, transcendentals=0),
        name=name,
    )(place, *operands)


def other_core(values):
    return lax.ppermute(values, "ch", [(i, i ^ 1) for i in range(2 * CHIPS)])


def receive_pieces(pieces):
    return [
        lax.ppermute(pieces[step], "ch", [(i, (i + 2 * step) % (2 * CHIPS)) for i in range(2 * CHIPS)])
        for step in STEPS[:-1]
    ]


def neighbour_rows(signal_ref, halo_ref, prev_ref, next_ref):
    values = signal_ref[...]
    width = values.shape[1]
    lanes = lax.broadcasted_iota(jnp.int32, values.shape, 1)
    prev_ref[...] = jnp.where(lanes == 0, halo_ref[:, 0:1], pltpu.roll(values, 1, 1))
    next_ref[...] = jnp.where(lanes == width - 1, halo_ref[:, 1:2], pltpu.roll(values, width - 1, 1))


def small_columns(values, at, prev, here, after, lane, first_step, last_step):
    lanes = lax.broadcasted_iota(jnp.int32, (values.shape[0], 128), 1)
    total = jnp.zeros((values.shape[0], 128), jnp.float32)
    for j, shifted in enumerate((prev, here, after)):
        total = jnp.where(lanes == lane + j, jnp.sum(values * shifted, axis=1, keepdims=True), total)
    first = jnp.where(at == first_step, values[:, :1], 0.0)
    last = jnp.where(at == last_step, values[:, -1:], 0.0)
    total = jnp.where(lanes == lane + 3, first, total)
    return jnp.where(lanes == lane + 4, last, total)


def output_kernel(
    tile_ref, block_ref, query_ref, cot_ref, signal_ref, halo_ref,
    out_ref, grad_ref, small_ref, level_ref, high_ref, low_ref, prev_ref, next_ref,
):
    at = pl.program_id(0)

    @pl.when(at == 0)
    def _():
        unpack(tile_ref, level_ref, 0)
        high_ref[...], low_ref[...] = split_two(level_ref[...])
        neighbour_rows(signal_ref, halo_ref, prev_ref, next_ref)

    mixed = dot_three((high_ref[...], low_ref[...]), split_two(block_ref[...]), 1, 1)
    out_ref[...] = query_ref[...] * mixed
    grad = cot_ref[...] * mixed
    grad_ref[...] = grad
    columns = pl.ds(pl.multiple_of(at * COLUMNS, COLUMNS), COLUMNS)
    small = small_columns(
        grad, at, prev_ref[:, columns], signal_ref[:, columns], next_ref[:, columns],
        0, 0, pl.num_programs(0) - 1,
    )

    @pl.when(at == 0)
    def _():
        small_ref[...] = small

    @pl.when(at > 0)
    def _():
        small_ref[...] += small


def make_output(tiles, block, query_conv, cotangent, signal, halo):
    breadth, height = signal.shape
    whole = lambda shape: pl.BlockSpec(shape, lambda i: (0,) * len(shape))
    strip = pl.BlockSpec((breadth, COLUMNS), lambda i: (0, i))
    full = jax.ShapeDtypeStruct(signal.shape, jnp.float32)
    return pl.pallas_call(
        output_kernel,
        grid=(height // COLUMNS,),
        out_shape=[full, full, jax.ShapeDtypeStruct((breadth, 128), jnp.float32)],
        in_specs=[
            whole(tiles.shape),
            pl.BlockSpec((COLUMNS, height), lambda i: (i, 0)),
            strip,
            strip,
            whole(signal.shape),
            whole(halo.shape),
        ],
        out_specs=[strip, strip, whole((breadth, 128))],
        scratch_shapes=[
            pltpu.VMEM(signal.shape, jnp.float32),
            pltpu.VMEM(signal.shape, jnp.bfloat16),
            pltpu.VMEM(signal.shape, jnp.bfloat16),
            pltpu.VMEM(signal.shape, jnp.float32),
            pltpu.VMEM(signal.shape, jnp.float32),
        ],
        compiler_params=pltpu.CompilerParams(vmem_limit_bytes=VMEM_LIMIT),
        cost_estimate=pl.CostEstimate(flops=1_200_000_000, bytes_accessed=9_000_000, transcendentals=0),
        name="make_output",
    )(tiles, block, query_conv, cotangent, signal, halo)


def gated_kernel(
    tile_ref, block_ref, key_ref, small_in_ref, signal_ref, halo_ref,
    own_ref, grad_ref, send_ref, level_ref, high_ref, low_ref, prev_ref, next_ref, small_ref,
):
    at = pl.program_id(0)
    steps = pl.num_programs(0)

    @pl.when(at == 0)
    def _():
        unpack(tile_ref, level_ref, 0)
        high_ref[...], low_ref[...] = split_two(level_ref[...])
        neighbour_rows(signal_ref, halo_ref, prev_ref, next_ref)
        small_ref[...] = small_in_ref[...]

    columns = pl.ds(pl.multiple_of(at * COLUMNS, COLUMNS), COLUMNS)
    here = signal_ref[:, columns]
    gated = dot_three((high_ref[...], low_ref[...]), split_two(block_ref[...]), 1, 0)
    own_ref[...] = gated * key_ref[...]
    grad = gated * here
    grad_ref[...] = grad
    small_ref[...] += small_columns(
        grad, at, prev_ref[:, columns], here, next_ref[:, columns], 5, 0, steps - 1
    )

    @pl.when(at == steps - 1)
    def _():
        rows = small_ref[...].T
        tail = jnp.concatenate([rows[0:5, 128:192], rows[5:10, 128:192]], axis=1)
        packed = jnp.concatenate([rows[0:10, 0:128], tail, jnp.zeros((1, 128), jnp.float32)], axis=0)
        for block in range(BLOCKS):
            send_ref[block] = packed


def make_gated(tiles, block, key_conv, small, signal, halo):
    breadth, height = signal.shape
    whole = lambda shape: pl.BlockSpec(shape, lambda i: (0,) * len(shape))
    strip = pl.BlockSpec((breadth, COLUMNS), lambda i: (0, i))
    full = jax.ShapeDtypeStruct(signal.shape, jnp.float32)
    send = (BLOCKS, 16, 128)
    return pl.pallas_call(
        gated_kernel,
        grid=(height // COLUMNS,),
        out_shape=[full, full, jax.ShapeDtypeStruct(send, jnp.float32)],
        in_specs=[
            whole(tiles.shape),
            pl.BlockSpec((height, COLUMNS), lambda i: (0, i)),
            strip,
            whole(small.shape),
            whole(signal.shape),
            whole(halo.shape),
        ],
        out_specs=[strip, strip, whole(send)],
        scratch_shapes=[
            pltpu.VMEM(signal.shape, jnp.float32),
            pltpu.VMEM(signal.shape, jnp.bfloat16),
            pltpu.VMEM(signal.shape, jnp.bfloat16),
            pltpu.VMEM(signal.shape, jnp.float32),
            pltpu.VMEM(signal.shape, jnp.float32),
            pltpu.VMEM((breadth, 128), jnp.float32),
        ],
        compiler_params=pltpu.CompilerParams(vmem_limit_bytes=VMEM_LIMIT),
        cost_estimate=pl.CostEstimate(flops=1_200_000_000, bytes_accessed=9_000_000, transcendentals=0),
        name="make_gated",
    )(tiles, block, key_conv, small, signal, halo)


def inside_kernel(own_ref, query_ref, key_ref, column_ref, mix_ref, out_ref, self_ref, partner_ref):
    total = own_ref[...]
    width = total.shape[1]
    lanes = lax.broadcasted_iota(jnp.int32, total.shape, 1)
    for rows_ref, tap in ((query_ref, 0), (key_ref, 3)):
        rows = rows_ref[...]
        ahead = jnp.where(lanes == width - 1, 0.0, pltpu.roll(rows, width - 1, 1))
        behind = jnp.where(lanes == 0, 0.0, pltpu.roll(rows, 1, 1))
        total = (
            total
            + column_ref[:, tap : tap + 1] * ahead
            + column_ref[:, tap + 1 : tap + 2] * rows
            + column_ref[:, tap + 2 : tap + 3] * behind
        )
    out_ref[...] = total
    mixes = []
    for group in range(16):
        mixes.append(mix_ref[2 * group] + mix_ref[2 * group + 1])
    for group in range(8):
        four = mix_ref[4 * group] + mix_ref[4 * group + 1] + mix_ref[4 * group + 2] + mix_ref[4 * group + 3]
        mixes.append(pltpu.roll(four, 64, 1))
    mixes = (jnp.concatenate(mixes, axis=0) * ROW_SCALE).T
    for section in range(SECTIONS):
        self_ref[section] = mixes[section : section + 1]
        partner_ref[section] = mixes[SECTIONS + section : SECTIONS + section + 1]


def make_inside(own, grad_query, grad_key, columns, mix_tiles):
    shape = jax.ShapeDtypeStruct(own.shape, jnp.float32)
    mix = jax.ShapeDtypeStruct((SECTIONS, 1, own.shape[0]), jnp.float32)
    return pl.pallas_call(
        inside_kernel,
        out_shape=[shape, mix, mix],
        in_specs=[pl.BlockSpec()] * 5,
        out_specs=[pl.BlockSpec()] * 3,
        compiler_params=pltpu.CompilerParams(vmem_limit_bytes=VMEM_LIMIT),
        cost_estimate=pl.CostEstimate(flops=3_000_000, bytes_accessed=4_000_000, transcendentals=0),
        name="make_inside",
    )(own, grad_query, grad_key, columns, mix_tiles)


def edge_kernel(block_ref, got_ref, column_ref, in_ref, out_ref, tap_q_ref, tap_k_ref):
    at = pl.program_id(0)
    block = block_ref[0]

    def table(packed):
        low = packed[0:10]
        high = jnp.concatenate([packed[10:15, 0:64], packed[10:15, 64:128]], axis=0)
        return jnp.concatenate([low, high], axis=1)

    def columns(packed):
        rows = table(packed)
        return jnp.concatenate([rows, jnp.zeros((118, 192), jnp.float32)], axis=0).T

    source = jnp.where(at == 0, jnp.maximum(block - 1, 0), jnp.minimum(block + 1, BLOCKS - 1))
    inside = jnp.where(at == 0, block > 0, block < BLOCKS - 1)
    halo = jnp.where(inside, columns(got_ref[source]), 0.0)
    lanes = lax.broadcasted_iota(jnp.int32, (192, 128), 1)

    @pl.when(at == 0)
    def _():
        extra = column_ref[:, 2:3] * halo[:, 4:5] + column_ref[:, 5:6] * halo[:, 9:10]
        out_ref[...] = in_ref[...] + jnp.where(lanes == 0, extra, 0.0)
        sums = table(jnp.sum(got_ref[...], axis=0)) * TOKEN_SCALE
        tap_q_ref[...] = sums[0:3]
        tap_k_ref[...] = sums[5:8]

    @pl.when(at == 1)
    def _():
        extra = column_ref[:, 0:1] * halo[:, 3:4] + column_ref[:, 3:4] * halo[:, 8:9]
        out_ref[...] = in_ref[...] + jnp.where(lanes == 127, extra, 0.0)


def make_edges(block, got, columns, inside):
    whole = lambda shape: pl.BlockSpec(shape, lambda i: (0,) * len(shape))
    last = inside.shape[1] // 128 - 1
    strip = pl.BlockSpec((inside.shape[0], 128), lambda i: (0, last * i))
    return pl.pallas_call(
        edge_kernel,
        grid=(2,),
        out_shape=[
            jax.ShapeDtypeStruct(inside.shape, jnp.float32),
            jax.ShapeDtypeStruct((3, inside.shape[0]), jnp.float32),
            jax.ShapeDtypeStruct((3, inside.shape[0]), jnp.float32),
        ],
        in_specs=[
            pl.BlockSpec(memory_space=pltpu.SMEM),
            whole(got.shape),
            whole(columns.shape),
            strip,
        ],
        out_specs=[strip] + [whole((3, inside.shape[0]))] * 2,
        input_output_aliases={3: 0},
        compiler_params=pltpu.CompilerParams(vmem_limit_bytes=VMEM_LIMIT),
        cost_estimate=pl.CostEstimate(flops=200_000, bytes_accessed=900_000, transcendentals=0),
        name="make_edges",
    )(block, got, columns, inside)


def local(signal, cotangent, kernel_q, kernel_k, block_first, block_second, mix_self, mix_partner):
    before, after = neighbours(signal[-1:], signal[:1])
    signal, cotangent = signal.T, cotangent.T
    columns = jnp.concatenate([kernel_q, kernel_k, mix_self[:, 0], mix_partner[:, 0]], axis=0).T
    swap = lambda tiles: lax.all_to_all(tiles, "seq", 0, 0, tiled=True)
    after_both = lax.optimization_barrier
    place = lax.axis_index("ch").reshape(1)
    block = lax.axis_index("seq").reshape(1)

    packed, gated_in, grad_mixed, query_conv, key_conv, halo = prologue(
        signal, cotangent, before, after, columns, block_first, block_second
    )
    incoming = swap(packed)
    gated_other, mixed_other = other_core(gated_in), other_core(grad_mixed)
    level_last = swap(butterfly_forward(incoming))
    grad_tiles = butterfly_backward(incoming)
    level_last, grad_tiles = after_both((level_last, grad_tiles))
    returned = swap(grad_tiles)

    level_other = other_core(level_last)
    pieces = block_products(
        second_kernel, (384, 1024), "block_second_products", place,
        grad_mixed, mixed_other, level_last, level_other,
    )
    level_last, pieces = after_both((level_last, pieces))
    output, grad_query, small = make_output(
        level_last, block_second[0], query_conv, cotangent, signal, halo
    )
    second_received = receive_pieces(pieces)
    second_own = pieces[0]
    returned, small, second_received[0] = after_both((returned, small, second_received[0]))

    returned_other = other_core(returned)
    pieces = block_products(
        first_kernel, (384, 128), "block_first_products", place,
        returned, returned_other, gated_in, gated_other,
    )
    returned, pieces = after_both((returned, pieces))
    first_received = receive_pieces(pieces)
    own, grad_key, send = make_gated(returned, block_first[0], key_conv, small, signal, halo)
    got = swap(send)
    inside, mix_self_grad, mix_partner_grad = make_inside(
        own, grad_query, grad_key, columns, returned[:, WEIGHT_TILE]
    )
    grad_second = second_own + second_received[0] + second_received[1] + second_received[2]
    grad_signal, tap_q_grad, tap_k_grad = make_edges(block, got, columns, inside)
    grad_first = pieces[0] + first_received[0] + first_received[1] + first_received[2]

    return (
        output.T,
        grad_signal.T,
        tap_q_grad,
        tap_k_grad,
        grad_first[None],
        grad_second[None],
        mix_self_grad,
        mix_partner_grad,
    )


def solution(mesh):
    return jax.shard_map(
        local,
        mesh=mesh,
        in_specs=(
            P("seq", "ch"),
            P("seq", "ch"),
            P(None, "ch"),
            P(None, "ch"),
            P("seq", None, None),
            P("seq", None, None),
            P(None, "seq", "ch"),
            P(None, "seq", "ch"),
        ),
        out_specs=(
            P("seq", "ch"),
            P("seq", "ch"),
            P(None, "ch"),
            P(None, "ch"),
            P("seq", "ch", None),
            P("seq", "ch", None),
            P(None, "seq", "ch"),
            P(None, "seq", "ch"),
        ),
        check_vma=False,
    )
```

```python
import math

import jax
import jax.numpy as jnp
from jax import lax
from jax.experimental import pallas as pl
from jax.experimental.pallas import tpu as pltpu
from jax.sharding import PartitionSpec as P

D = 1536
SECTIONS = 5
BLOCKS = 32
PARTS = ((0, 4), (4, 6))
LANE_OF_PART = (0, 64)
WEIGHT_TILE = 6
CHIPS = 4
STEPS = (2, 1, 3, 0)
COLUMNS = 256
VMEM_LIMIT = 56 * 1024 * 1024
WIDTH_SCALE = 1.0 / math.sqrt(D)
ROW_SCALE = 1.0 / math.sqrt(1024)
TOKEN_SCALE = 1.0 / math.sqrt(32768)

def flip(values, section):
    stride = 2**section
    pieces = []
    for at in range(0, BLOCKS, 2 * stride):
        pieces.append(values[at + stride : at + 2 * stride])
        pieces.append(values[at : at + stride])
    return jnp.concatenate(pieces, axis=0)


def load_weights(in_ref, weight_ref):
    for part in range(2):
        for at in range(2 * SECTIONS):
            lane = LANE_OF_PART[part] + at
            column = in_ref[:, 12, :, lane : lane + 1]
            weight_ref[part, at] = jnp.broadcast_to(column, (BLOCKS, 8, 128))


def step_forward(level, weight_ref, part, section):
    return (
        weight_ref[part, section] * level
        + weight_ref[part, SECTIONS + section] * flip(level, section)
    )


def forward_kernel(in_ref, out_ref, weight_ref):
    load_weights(in_ref, weight_ref)
    for part, (low, high) in enumerate(PARTS):

        def one_tile(tile, carry):
            level = in_ref[:, tile]
            for section in range(SECTIONS):
                level = step_forward(level, weight_ref, part, section)
            out_ref[:, tile] = level
            return carry

        lax.fori_loop(low, high, one_tile, 0)


def backward_kernel(in_ref, out_ref, weight_ref, level_ref, sum_ref):
    load_weights(in_ref, weight_ref)
    for part, (low, high) in enumerate(PARTS):

        def one_tile(tile, first):
            level = in_ref[:, tile]
            for section in range(SECTIONS):
                level_ref[section] = level
                if section < SECTIONS - 1:
                    level = step_forward(level, weight_ref, part, section)
            grad = in_ref[:, 6 + tile]
            for section in reversed(range(SECTIONS)):
                level = level_ref[section]
                own = grad * level
                other = grad * flip(level, section)
                if first:
                    sum_ref[part, section] = own
                    sum_ref[part, SECTIONS + section] = other
                else:
                    sum_ref[part, section] += own
                    sum_ref[part, SECTIONS + section] += other
                grad = weight_ref[part, section] * grad + flip(
                    weight_ref[part, SECTIONS + section] * grad, section
                )
            out_ref[:, tile] = grad

        one_tile(low, True)

        def body(tile, carry):
            one_tile(tile, False)
            return carry

        lax.fori_loop(low + 1, high, body, 0)

    lanes = lax.broadcasted_iota(jnp.int32, (BLOCKS, 8, 128), 2)
    result = jnp.zeros((BLOCKS, 8, 128), jnp.float32)
    for part in range(2):
        for at in range(2 * SECTIONS):
            total = jnp.sum(sum_ref[part, at], axis=2, keepdims=True)
            result = jnp.where(lanes == LANE_OF_PART[part] + at, total, result)
    out_ref[:, WEIGHT_TILE] = result


WEIGHT_SCRATCH = (2, 2 * SECTIONS, BLOCKS, 8, 128)
IN_VMEM = pl.BlockSpec(memory_space=pltpu.VMEM)


def butterfly_forward(tiles):
    return pl.pallas_call(
        forward_kernel,
        out_shape=jax.ShapeDtypeStruct((BLOCKS, 6, 8, 128), jnp.float32),
        in_specs=[IN_VMEM],
        out_specs=IN_VMEM,
        scratch_shapes=[pltpu.VMEM(WEIGHT_SCRATCH, jnp.float32)],
        compiler_params=pltpu.CompilerParams(vmem_limit_bytes=24 * 1024 * 1024),
        cost_estimate=pl.CostEstimate(flops=4_000_000, bytes_accessed=1_800_000, transcendentals=0),
        name="butterfly_forward",
    )(tiles)


def butterfly_backward(tiles):
    return pl.pallas_call(
        backward_kernel,
        out_shape=jax.ShapeDtypeStruct((BLOCKS, 7, 8, 128), jnp.float32),
        in_specs=[IN_VMEM],
        out_specs=IN_VMEM,
        scratch_shapes=[
            pltpu.VMEM(WEIGHT_SCRATCH, jnp.float32),
            pltpu.VMEM((SECTIONS, BLOCKS, 8, 128), jnp.float32),
            pltpu.VMEM(WEIGHT_SCRATCH, jnp.float32),
        ],
        compiler_params=pltpu.CompilerParams(vmem_limit_bytes=32 * 1024 * 1024),
        cost_estimate=pl.CostEstimate(flops=12_000_000, bytes_accessed=2_600_000, transcendentals=0),
        name="butterfly_backward",
    )(tiles)


def neighbours(low, high):
    count = lax.axis_size("seq")
    before = lax.ppermute(low, "seq", [(i, i + 1) for i in range(count - 1)])
    after = lax.ppermute(high, "seq", [(i + 1, i) for i in range(count - 1)])
    return before, after


def owner_and_tile(group, chunk):
    if group < 16:
        return 2 * group + chunk // 4, chunk % 4
    return 4 * (group - 16) + chunk // 2, 4 + chunk % 2


def split_two(values):
    high = values.astype(jnp.bfloat16)
    return high, (values - high.astype(jnp.float32)).astype(jnp.bfloat16)


def dot_three(left, right, left_dim, right_dim):
    def dot(a, b):
        return lax.dot_general(
            a, b, (((left_dim,), (right_dim,)), ((), ())), preferred_element_type=jnp.float32
        )

    (left_high, left_low), (right_high, right_low) = left, right
    return dot(left_high, right_high) + (dot(left_high, right_low) + dot(left_low, right_high))


def unpack(tile_ref, dest_ref, row):
    for group in range(24):
        for chunk in range(8):
            owner, tile = owner_and_tile(group, chunk)
            dest_ref[row + 8 * group : row + 8 * group + 8, 128 * chunk : 128 * chunk + 128] = (
                tile_ref[owner, tile]
            )


def chunk_of_step(place_ref, step):
    place = place_ref[0]
    return 2 * ((place // 2 + step) % CHIPS) + place % 2


def second_kernel(place_ref, left_a, left_b, right_a, right_b, *refs):
    outs, (right_ref,) = refs[:CHIPS], refs[CHIPS:]
    unpack(right_a, right_ref, 0)
    unpack(right_b, right_ref, 192)
    right = split_two(right_ref[...])
    for step in STEPS:
        rows = pl.ds(pl.multiple_of(chunk_of_step(place_ref, step) * 128, 128), 128)
        left = jnp.concatenate([left_a[:, rows], left_b[:, rows]], axis=0) * WIDTH_SCALE
        outs[step][...] = dot_three(split_two(left), right, 0, 0)


def first_kernel(place_ref, tiles_a, tiles_b, right_a, right_b, *refs):
    outs, (left_ref, tile_ref, right_ref, sem) = refs[:CHIPS], refs[CHIPS:]
    copies = []
    for half, (tiles, right) in enumerate(((tiles_a, right_a), (tiles_b, right_b))):
        copies.append(pltpu.make_async_copy(right, right_ref.at[half], sem.at[2 * half]))
        copies.append(pltpu.make_async_copy(tiles, tile_ref.at[half], sem.at[2 * half + 1]))
    for copy in copies:
        copy.start()
    for half in range(2):
        copies[2 * half].wait()
        right = split_two(right_ref[half])
        copies[2 * half + 1].wait()
        for step in STEPS:
            chunk = chunk_of_step(place_ref, step)
            for group in range(24):
                owner, tile = owner_and_tile(group, chunk)
                left_ref[step, 8 * group : 8 * group + 8, :] = tile_ref[half, owner, tile]
            product = dot_three(split_two(left_ref[step] * WIDTH_SCALE), right, 0, 0)
            if half == 0:
                outs[step][...] = product
            else:
                outs[step][...] += product


def first_products(place, tiles, tiles_other, gated, gated_other):
    piece = jax.ShapeDtypeStruct((128, 1024), jnp.float32)
    return pl.pallas_call(
        first_kernel,
        out_shape=[piece] * CHIPS,
        in_specs=[pl.BlockSpec(memory_space=pltpu.SMEM)] + [IN_HBM] * 4,
        out_specs=[pl.BlockSpec()] * CHIPS,
        scratch_shapes=[
            pltpu.VMEM((CHIPS, 192, 128), jnp.float32),
            pltpu.VMEM((2,) + tiles.shape, jnp.float32),
            pltpu.VMEM((2,) + gated.shape, jnp.float32),
            pltpu.SemaphoreType.DMA((4,)),
        ],
        compiler_params=pltpu.CompilerParams(vmem_limit_bytes=VMEM_LIMIT),
        cost_estimate=pl.CostEstimate(flops=1_200_000_000, bytes_accessed=5_000_000, transcendentals=0),
        name="block_first_products",
    )(place, tiles, tiles_other, gated, gated_other)


def shifted(values, before, after):
    width = values.shape[1]
    lanes = lax.broadcasted_iota(jnp.int32, values.shape, 1)
    prev = jnp.where(lanes == 0, before, pltpu.roll(values, 1, 1))
    return prev, jnp.where(lanes == width - 1, after, pltpu.roll(values, width - 1, 1))


def conv(column_ref, tap, prev, values, later):
    return (
        column_ref[:, tap : tap + 1] * prev
        + column_ref[:, tap + 1 : tap + 2] * values
        + column_ref[:, tap + 2 : tap + 3] * later
    )


def strips(ref, buffer, sem, first, along):
    copies = []
    for at in range(4):
        part = pl.ds(256 * at, 256)
        index = (part, slice(None)) if along == 0 else (slice(None), part)
        copies.append(pltpu.make_async_copy(ref.at[index], buffer.at[index], sem.at[first + at]))
    return copies


IN_HBM = pl.BlockSpec(memory_space=pl.ANY)


def prologue_kernel(
    signal_ref, cot_ref, before_ref, after_ref, taps_q_ref, taps_k_ref, self_ref, partner_ref, first_ref, second_ref,
    packed_ref, gated_ref, mixed_ref, halo_ref, column_ref,
    gated_high, gated_low, mixed_high, mixed_low,
):
    at = pl.program_id(0)

    @pl.when(at == 0)
    def _():
        values = signal_ref[...]
        rows = [taps_q_ref[...], taps_k_ref[...]]
        rows += [ref[section] for ref in (self_ref, partner_ref) for section in range(SECTIONS)]
        rows.append(jnp.zeros((112, values.shape[0]), jnp.float32))
        column_ref[...] = jnp.concatenate(rows, axis=0).T
        before = jnp.broadcast_to(before_ref[...], (128, values.shape[0])).T
        after = jnp.broadcast_to(after_ref[...], (128, values.shape[0])).T
        narrow = lax.broadcasted_iota(jnp.int32, before.shape, 1)
        halo_ref[...] = jnp.where(narrow == 0, before, after)
        prev, later = shifted(values, before[:, :1], after[:, :1])
        gated = conv(column_ref, 3, prev, values, later) * values
        gated_ref[...] = gated
        gated_high[...], gated_low[...] = split_two(gated)
        mixed = cot_ref[...] * conv(column_ref, 0, prev, values, later)
        mixed_ref[...] = mixed
        mixed_high[...], mixed_low[...] = split_two(mixed)
        weights = jnp.concatenate(
            [column_ref[:, 6:16], jnp.zeros((values.shape[0], 118), jnp.float32)], axis=1
        )
        moved = pltpu.roll(weights[128:192], 64, 1)
        for owner in range(BLOCKS):
            low, high = 8 * (owner // 2), 8 * (owner // 4)
            packed_ref[owner, 12] = weights[low : low + 8] + moved[high : high + 8]

    level = dot_three((gated_high[...], gated_low[...]), split_two(first_ref[0]), 1, 1)
    grad = dot_three((mixed_high[...], mixed_low[...]), split_two(second_ref[0]), 1, 0)
    for part in range(COLUMNS // 128):
        chunk = at * (COLUMNS // 128) + part
        for group in range(24):
            owner, tile = owner_and_tile(group, chunk)
            rows, lanes = slice(8 * group, 8 * group + 8), slice(128 * part, 128 * part + 128)
            packed_ref[owner, tile] = level[rows, lanes]
            packed_ref[owner, 6 + tile] = grad[rows, lanes]


def prologue(signal, cotangent, before, after, taps_q, taps_k, mix_self, mix_partner, first, second):
    breadth, height = signal.shape
    whole = lambda shape: pl.BlockSpec(shape, lambda i: (0,) * len(shape))
    full = jax.ShapeDtypeStruct(signal.shape, jnp.float32)
    packed = (BLOCKS, 13, 8, 128)
    return pl.pallas_call(
        prologue_kernel,
        grid=(height // COLUMNS,),
        out_shape=[jax.ShapeDtypeStruct(packed, jnp.float32)]
        + [full] * 2
        + [jax.ShapeDtypeStruct((breadth, 128), jnp.float32)] * 2,
        in_specs=[
            whole(signal.shape),
            whole(signal.shape),
            whole(before.shape),
            whole(after.shape),
            whole(taps_q.shape),
            whole(taps_k.shape),
            whole(mix_self.shape),
            whole(mix_partner.shape),
            pl.BlockSpec((1, COLUMNS, height), lambda i: (0, i, 0)),
            pl.BlockSpec((1, height, COLUMNS), lambda i: (0, 0, i)),
        ],
        out_specs=[whole(packed)] + [whole(signal.shape)] * 2 + [whole((breadth, 128))] * 2,
        scratch_shapes=[pltpu.VMEM(signal.shape, jnp.bfloat16)] * 4,
        compiler_params=pltpu.CompilerParams(vmem_limit_bytes=VMEM_LIMIT),
        cost_estimate=pl.CostEstimate(flops=2_400_000_000, bytes_accessed=15_000_000, transcendentals=0),
        name="prologue",
    )(signal, cotangent, before, after, taps_q, taps_k, mix_self, mix_partner, first, second)


def block_products(kernel, scratch, name, place, *operands):
    piece = jax.ShapeDtypeStruct((128, 1024), jnp.float32)
    return pl.pallas_call(
        kernel,
        out_shape=[piece] * CHIPS,
        in_specs=[pl.BlockSpec(memory_space=pltpu.SMEM)] + [pl.BlockSpec()] * 4,
        out_specs=[pl.BlockSpec()] * CHIPS,
        scratch_shapes=[pltpu.VMEM(scratch, jnp.float32)],
        compiler_params=pltpu.CompilerParams(vmem_limit_bytes=VMEM_LIMIT),
        cost_estimate=pl.CostEstimate(flops=1_200_000_000, bytes_accessed=5_000_000, transcendentals=0),
        name=name,
    )(place, *operands)


def other_core(values):
    return lax.ppermute(values, "ch", [(i, i ^ 1) for i in range(2 * CHIPS)])


def receive_pieces(pieces):
    return [
        lax.ppermute(pieces[step], "ch", [(i, (i + 2 * step) % (2 * CHIPS)) for i in range(2 * CHIPS)])
        for step in STEPS[:-1]
    ]


def tap_products(values, prev, here, later):
    out = []
    for other in (prev, here, later):
        product = values * other
        total = product[:, :128]
        for at in range(128, product.shape[1], 128):
            total = total + product[:, at : at + 128]
        out.append(total)
    return out


def small_columns(sums, first, last, lane):
    lanes = lax.broadcasted_iota(jnp.int32, sums[0].shape, 1)
    total = jnp.zeros(sums[0].shape, jnp.float32)
    for j, value in enumerate(sums):
        total = jnp.where(lanes == lane + j, jnp.sum(value, axis=1, keepdims=True), total)
    total = jnp.where(lanes == lane + 3, first, total)
    return jnp.where(lanes == lane + 4, last, total)


def output_kernel(
    column_ref, halo_ref, tile_hbm, block_hbm, signal_hbm, cot_hbm,
    out_hbm, grad_hbm, small_ref,
    tile_ref, block_ref, signal_ref, cot_ref, level_ref, out_ref, grad_ref, sem,
):
    get_tiles = pltpu.make_async_copy(tile_hbm, tile_ref, sem.at[0])
    get_signal = pltpu.make_async_copy(signal_hbm, signal_ref, sem.at[1])
    get_cot = pltpu.make_async_copy(cot_hbm, cot_ref, sem.at[2])
    get_block = strips(block_hbm.at[0], block_ref, sem, 3, 0)
    get_tiles.start()
    get_signal.start()
    get_block[0].start()
    get_cot.start()
    for copy in get_block[1:]:
        copy.start()
    get_tiles.wait()
    unpack(tile_ref, level_ref, 0)
    left = split_two(level_ref[...])
    get_signal.wait()
    values = signal_ref[...]
    prev, later = shifted(values, halo_ref[:, 0:1], halo_ref[:, 1:2])
    query = conv(column_ref, 0, prev, values, later)
    sums, puts = None, []
    for at in range(4):
        part = slice(256 * at, 256 * at + 256)
        get_block[at].wait()
        mixed = dot_three(left, split_two(block_ref[part, :]), 1, 1)
        if at == 0:
            get_cot.wait()
        out_ref[:, part] = query[:, part] * mixed
        grad = cot_ref[:, part] * mixed
        grad_ref[:, part] = grad
        for index, (ref, hbm) in enumerate(((out_ref, out_hbm), (grad_ref, grad_hbm))):
            put = pltpu.make_async_copy(ref.at[:, part], hbm.at[:, part], sem.at[7 + 2 * at + index])
            put.start()
            puts.append(put)
        new = tap_products(grad, prev[:, part], values[:, part], later[:, part])
        sums = new if sums is None else [a + b for a, b in zip(sums, new)]
    small_ref[...] = small_columns(sums, grad_ref[:, 0:1], grad_ref[:, 1023:1024], 0)
    for put in puts:
        put.wait()


def make_output(tiles, block, cotangent, signal, columns, halo):
    full = jax.ShapeDtypeStruct(signal.shape, jnp.float32)
    buffer = pltpu.VMEM(signal.shape, jnp.float32)
    return pl.pallas_call(
        output_kernel,
        out_shape=[full, full, jax.ShapeDtypeStruct((signal.shape[0], 128), jnp.float32)],
        in_specs=[pl.BlockSpec()] * 2 + [IN_HBM] * 4,
        out_specs=[IN_HBM] * 2 + [pl.BlockSpec()],
        scratch_shapes=[
            pltpu.VMEM(tiles.shape, jnp.float32),
            pltpu.VMEM(block.shape[1:], jnp.float32),
            buffer,
            buffer,
            buffer,
            buffer,
            buffer,
            pltpu.SemaphoreType.DMA((15,)),
        ],
        compiler_params=pltpu.CompilerParams(vmem_limit_bytes=VMEM_LIMIT),
        cost_estimate=pl.CostEstimate(flops=1_200_000_000, bytes_accessed=9_000_000, transcendentals=0),
        name="make_output",
    )(columns, halo, tiles, block, signal, cotangent)


def tap_kernel(halo_ref, signal_ref, block_ref, out_ref, ends_ref, edge_ref, high_ref, low_ref):
    at = pl.program_id(0)
    breadth = signal_ref.shape[0]

    @pl.when(at == 0)
    def _():
        values = signal_ref[...]
        prev, later = shifted(values, halo_ref[:, 0:1], halo_ref[:, 1:2])
        for j, other in enumerate((prev, values, later)):
            rows = slice(breadth * j, breadth * j + breadth)
            high_ref[rows, :], low_ref[rows, :] = split_two(values * other)
        lanes = lax.broadcasted_iota(jnp.int32, (breadth, 128), 1)
        ends_ref[...] = jnp.where(lanes == 0, values[:, :1], values[:, 1023:1024])

    block = block_ref[0]
    out_ref[...] = dot_three((high_ref[...], low_ref[...]), split_two(block), 1, 1)
    first = block[:, 0:128].T
    last = block[:, 896:1024].T
    edge_ref[0:8, :] = jnp.broadcast_to(first[0:1], (8, first.shape[1]))
    edge_ref[8:16, :] = jnp.broadcast_to(last[127:128], (8, first.shape[1]))


def tap_weights(signal, halo, block):
    breadth, height = signal.shape
    whole = lambda shape: pl.BlockSpec(shape, lambda i: (0,) * len(shape))
    return pl.pallas_call(
        tap_kernel,
        grid=(height // COLUMNS,),
        out_shape=[
            jax.ShapeDtypeStruct((3 * breadth, height), jnp.float32),
            jax.ShapeDtypeStruct((breadth, 128), jnp.float32),
            jax.ShapeDtypeStruct((16, height), jnp.float32),
        ],
        in_specs=[
            whole(halo.shape),
            whole(signal.shape),
            pl.BlockSpec((1, COLUMNS, height), lambda i: (0, i, 0)),
        ],
        out_specs=[
            pl.BlockSpec((3 * breadth, COLUMNS), lambda i: (0, i)),
            whole((breadth, 128)),
            pl.BlockSpec((16, COLUMNS), lambda i: (0, i)),
        ],
        scratch_shapes=[pltpu.VMEM((3 * breadth, height), jnp.bfloat16)] * 2,
        compiler_params=pltpu.CompilerParams(vmem_limit_bytes=VMEM_LIMIT),
        cost_estimate=pl.CostEstimate(flops=3_600_000_000, bytes_accessed=8_000_000, transcendentals=0),
        name="tap_weights",
    )(halo, signal, block)


def send_kernel(tile_ref, weight_ref, ends_ref, edge_ref, small_in_ref, send_ref):
    breadth = ends_ref.shape[0]
    totals = [[] for _ in range(5)]
    for group in range(24):
        sums = [None] * 5
        for chunk in range(8):
            owner, tile = owner_and_tile(group, chunk)
            values = tile_ref[owner, tile]
            lanes = slice(128 * chunk, 128 * chunk + 128)
            others = [
                weight_ref[breadth * j + 8 * group : breadth * j + 8 * group + 8, lanes] for j in range(3)
            ] + [edge_ref[0:8, lanes], edge_ref[8:16, lanes]]
            for j, other in enumerate(others):
                product = values * other
                sums[j] = product if sums[j] is None else sums[j] + product
        for j in range(5):
            totals[j].append(sums[j])
    lanes = lax.broadcasted_iota(jnp.int32, (breadth, 128), 1)
    small = small_in_ref[...]
    for j in range(5):
        total = jnp.sum(jnp.concatenate(totals[j], axis=0), axis=1, keepdims=True)
        if j >= 3:
            total = total * ends_ref[:, j - 3 : j - 2]
        small = small + jnp.where(lanes == 5 + j, total, 0.0)
    rows = small.T
    tail = jnp.concatenate([rows[0:5, 128:192], rows[5:10, 128:192]], axis=1)
    packed = jnp.concatenate([rows[0:10, 0:128], tail, jnp.zeros((1, 128), jnp.float32)], axis=0)
    for block in range(BLOCKS):
        send_ref[block] = packed


def make_send(tiles, weights, ends, edges, small):
    return pl.pallas_call(
        send_kernel,
        out_shape=jax.ShapeDtypeStruct((BLOCKS, 16, 128), jnp.float32),
        in_specs=[pl.BlockSpec()] * 5,
        out_specs=pl.BlockSpec(),
        compiler_params=pltpu.CompilerParams(vmem_limit_bytes=VMEM_LIMIT),
        cost_estimate=pl.CostEstimate(flops=2_000_000, bytes_accessed=4_000_000, transcendentals=0),
        name="make_send",
    )(tiles, weights, ends, edges, small)


def inside_kernel(
    halo_ref, column_ref, tile_hbm, block_hbm, signal_hbm, query_hbm,
    out_hbm, self_ref, partner_ref,
    tile_ref, block_ref, signal_ref, query_ref, level_ref, gated_ref, sem,
):
    get_tiles = pltpu.make_async_copy(tile_hbm, tile_ref, sem.at[0])
    get_signal = pltpu.make_async_copy(signal_hbm, signal_ref, sem.at[1])
    get_query = pltpu.make_async_copy(query_hbm, query_ref, sem.at[2])
    get_block = strips(block_hbm.at[0], block_ref, sem, 3, 1)
    get_tiles.start()
    for copy in get_block:
        copy.start()
    get_signal.start()
    get_query.start()
    get_tiles.wait()
    unpack(tile_ref, level_ref, 0)
    left = split_two(level_ref[...])
    for at in range(4):
        part = slice(256 * at, 256 * at + 256)
        get_block[at].wait()
        gated_ref[:, part] = dot_three(left, split_two(block_ref[:, part]), 1, 0)
    get_signal.wait()
    get_query.wait()
    values, gated = signal_ref[...], gated_ref[...]
    prev, later = shifted(values, halo_ref[:, 0:1], halo_ref[:, 1:2])
    total = gated * conv(column_ref, 3, prev, values, later)
    for rows, tap in ((query_ref[...], 0), (gated * values, 3)):
        behind, ahead = shifted(rows, 0.0, 0.0)
        total = total + conv(column_ref, tap, ahead, rows, behind)
    level_ref[...] = total
    put = pltpu.make_async_copy(level_ref, out_hbm, sem.at[7])
    put.start()
    mix_ref = tile_ref.at[:, WEIGHT_TILE]
    mixes = []
    for group in range(16):
        mixes.append(mix_ref[2 * group] + mix_ref[2 * group + 1])
    for group in range(8):
        four = mix_ref[4 * group] + mix_ref[4 * group + 1] + mix_ref[4 * group + 2] + mix_ref[4 * group + 3]
        mixes.append(pltpu.roll(four, 64, 1))
    mixes = (jnp.concatenate(mixes, axis=0) * ROW_SCALE).T
    for section in range(SECTIONS):
        self_ref[section] = mixes[section : section + 1]
        partner_ref[section] = mixes[SECTIONS + section : SECTIONS + section + 1]
    put.wait()


def make_inside(tiles, block, signal, grad_query, halo, columns):
    mix = jax.ShapeDtypeStruct((SECTIONS, 1, signal.shape[0]), jnp.float32)
    buffer = pltpu.VMEM(signal.shape, jnp.float32)
    return pl.pallas_call(
        inside_kernel,
        out_shape=[jax.ShapeDtypeStruct(signal.shape, jnp.float32), mix, mix],
        in_specs=[pl.BlockSpec()] * 2 + [IN_HBM] * 4,
        out_specs=[IN_HBM] + [pl.BlockSpec()] * 2,
        scratch_shapes=[
            pltpu.VMEM(tiles.shape, jnp.float32),
            pltpu.VMEM(block.shape[1:], jnp.float32),
            buffer,
            buffer,
            buffer,
            buffer,
            pltpu.SemaphoreType.DMA((8,)),
        ],
        compiler_params=pltpu.CompilerParams(vmem_limit_bytes=VMEM_LIMIT),
        cost_estimate=pl.CostEstimate(flops=1_200_000_000, bytes_accessed=8_000_000, transcendentals=0),
        name="make_inside",
    )(halo, columns, tiles, block, signal, grad_query)


def edge_kernel(block_ref, got_ref, column_ref, in_ref, out_ref, tap_q_ref, tap_k_ref):
    at = pl.program_id(0)
    block = block_ref[0]

    def table(packed):
        low = packed[0:10]
        high = jnp.concatenate([packed[10:15, 0:64], packed[10:15, 64:128]], axis=0)
        return jnp.concatenate([low, high], axis=1)

    def columns(packed):
        rows = table(packed)
        return jnp.concatenate([rows, jnp.zeros((118, 192), jnp.float32)], axis=0).T

    source = jnp.where(at == 0, jnp.maximum(block - 1, 0), jnp.minimum(block + 1, BLOCKS - 1))
    inside = jnp.where(at == 0, block > 0, block < BLOCKS - 1)
    halo = jnp.where(inside, columns(got_ref[source]), 0.0)
    lanes = lax.broadcasted_iota(jnp.int32, (192, 128), 1)

    @pl.when(at == 0)
    def _():
        extra = column_ref[:, 2:3] * halo[:, 4:5] + column_ref[:, 5:6] * halo[:, 9:10]
        out_ref[...] = in_ref[...] + jnp.where(lanes == 0, extra, 0.0)
        sums = table(jnp.sum(got_ref[...], axis=0)) * TOKEN_SCALE
        tap_q_ref[...] = sums[0:3]
        tap_k_ref[...] = sums[5:8]

    @pl.when(at == 1)
    def _():
        extra = column_ref[:, 0:1] * halo[:, 3:4] + column_ref[:, 3:4] * halo[:, 8:9]
        out_ref[...] = in_ref[...] + jnp.where(lanes == 127, extra, 0.0)


def make_edges(block, got, columns, inside):
    whole = lambda shape: pl.BlockSpec(shape, lambda i: (0,) * len(shape))
    last = inside.shape[1] // 128 - 1
    strip = pl.BlockSpec((inside.shape[0], 128), lambda i: (0, last * i))
    return pl.pallas_call(
        edge_kernel,
        grid=(2,),
        out_shape=[
            jax.ShapeDtypeStruct(inside.shape, jnp.float32),
            jax.ShapeDtypeStruct((3, inside.shape[0]), jnp.float32),
            jax.ShapeDtypeStruct((3, inside.shape[0]), jnp.float32),
        ],
        in_specs=[
            pl.BlockSpec(memory_space=pltpu.SMEM),
            whole(got.shape),
            whole(columns.shape),
            strip,
        ],
        out_specs=[strip] + [whole((3, inside.shape[0]))] * 2,
        input_output_aliases={3: 0},
        compiler_params=pltpu.CompilerParams(vmem_limit_bytes=VMEM_LIMIT),
        cost_estimate=pl.CostEstimate(flops=200_000, bytes_accessed=900_000, transcendentals=0),
        name="make_edges",
    )(block, got, columns, inside)


def local(signal, cotangent, kernel_q, kernel_k, block_first, block_second, mix_self, mix_partner):
    before, after = neighbours(signal[-1:], signal[:1])
    signal, cotangent = signal.T, cotangent.T
    swap = lambda tiles: lax.all_to_all(tiles, "seq", 0, 0, tiled=True)
    after_both = lax.optimization_barrier
    place = lax.axis_index("ch").reshape(1)
    block = lax.axis_index("seq").reshape(1)

    packed, gated_in, grad_mixed, halo, columns = prologue(
        signal, cotangent, before, after, kernel_q, kernel_k, mix_self, mix_partner,
        block_first, block_second,
    )
    incoming = swap(packed)
    gated_other, mixed_other = other_core(gated_in), other_core(grad_mixed)
    level_last = swap(butterfly_forward(incoming))
    grad_tiles = butterfly_backward(incoming)
    tap_parts = tap_weights(signal, halo, block_first)
    level_last, grad_tiles, tap_parts = after_both((level_last, grad_tiles, tap_parts))
    returned = swap(grad_tiles)

    level_other = other_core(level_last)
    pieces = block_products(
        second_kernel, (384, 1024), "block_second_products", place,
        grad_mixed, mixed_other, level_last, level_other,
    )
    level_last, pieces = after_both((level_last, pieces))
    output, grad_query, small = make_output(
        level_last, block_second, cotangent, signal, columns, halo
    )
    second_received = receive_pieces(pieces)
    second_own = pieces[0]
    returned, small, second_received[1:] = after_both((returned, small, second_received[1:]))

    returned_other = other_core(returned)
    send = make_send(returned, *tap_parts, small)
    returned_other, send = after_both((returned_other, send))
    pieces = first_products(place, returned, returned_other, gated_in, gated_other)
    first_received = receive_pieces(pieces)
    send, pieces = after_both((send, pieces))
    got = swap(send)
    inside, mix_self_grad, mix_partner_grad = make_inside(
        returned, block_first, signal, grad_query, halo, columns
    )
    grad_second = second_own + second_received[0] + second_received[1] + second_received[2]
    grad_signal, tap_q_grad, tap_k_grad = make_edges(block, got, columns, inside)
    grad_first = pieces[0] + first_received[0] + first_received[1] + first_received[2]

    return (
        output.T,
        grad_signal.T,
        tap_q_grad,
        tap_k_grad,
        grad_first[None],
        grad_second[None],
        mix_self_grad,
        mix_partner_grad,
    )


def solution(mesh):
    return jax.shard_map(
        local,
        mesh=mesh,
        in_specs=(
            P("seq", "ch"),
            P("seq", "ch"),
            P(None, "ch"),
            P(None, "ch"),
            P("seq", None, None),
            P("seq", None, None),
            P(None, "seq", "ch"),
            P(None, "seq", "ch"),
        ),
        out_specs=(
            P("seq", "ch"),
            P("seq", "ch"),
            P(None, "ch"),
            P(None, "ch"),
            P("seq", "ch", None),
            P("seq", "ch", None),
            P(None, "seq", "ch"),
            P(None, "seq", "ch"),
        ),
        check_vma=False,
    )
```

```python
import math

import jax
import jax.numpy as jnp
from jax import lax
from jax.experimental import pallas as pl
from jax.experimental.pallas import tpu as pltpu
from jax.sharding import PartitionSpec as P

D = 1536
SECTIONS = 5
BLOCKS = 32
PARTS = ((0, 4), (4, 6))
LANE_OF_PART = (0, 64)
WEIGHT_TILE = 6
CHIPS = 4
STEPS = (2, 1, 3, 0)
COLUMNS = 256
VMEM_LIMIT = 56 * 1024 * 1024
WIDTH_SCALE = 1.0 / math.sqrt(D)
ROW_SCALE = 1.0 / math.sqrt(1024)
TOKEN_SCALE = 1.0 / math.sqrt(32768)

def flip(values, section):
    stride = 2**section
    pieces = []
    for at in range(0, BLOCKS, 2 * stride):
        pieces.append(values[at + stride : at + 2 * stride])
        pieces.append(values[at : at + stride])
    return jnp.concatenate(pieces, axis=0)


def load_weights(in_ref, weight_ref):
    for part in range(2):
        for at in range(2 * SECTIONS):
            lane = LANE_OF_PART[part] + at
            column = in_ref[:, 12, :, lane : lane + 1]
            weight_ref[part, at] = jnp.broadcast_to(column, (BLOCKS, 8, 128))


def step_forward(level, weight_ref, part, section):
    return (
        weight_ref[part, section] * level
        + weight_ref[part, SECTIONS + section] * flip(level, section)
    )


def forward_kernel(in_ref, out_ref, weight_ref):
    load_weights(in_ref, weight_ref)
    for part, (low, high) in enumerate(PARTS):

        def one_tile(tile, carry):
            level = in_ref[:, tile]
            for section in range(SECTIONS):
                level = step_forward(level, weight_ref, part, section)
            out_ref[:, tile] = level
            return carry

        lax.fori_loop(low, high, one_tile, 0)


def backward_kernel(in_ref, out_ref, weight_ref, level_ref, sum_ref):
    load_weights(in_ref, weight_ref)
    for part, (low, high) in enumerate(PARTS):

        def one_tile(tile, first):
            level = in_ref[:, tile]
            for section in range(SECTIONS):
                level_ref[section] = level
                if section < SECTIONS - 1:
                    level = step_forward(level, weight_ref, part, section)
            grad = in_ref[:, 6 + tile]
            for section in reversed(range(SECTIONS)):
                level = level_ref[section]
                own = grad * level
                other = grad * flip(level, section)
                if first:
                    sum_ref[part, section] = own
                    sum_ref[part, SECTIONS + section] = other
                else:
                    sum_ref[part, section] += own
                    sum_ref[part, SECTIONS + section] += other
                grad = weight_ref[part, section] * grad + flip(
                    weight_ref[part, SECTIONS + section] * grad, section
                )
            out_ref[:, tile] = grad

        one_tile(low, True)

        def body(tile, carry):
            one_tile(tile, False)
            return carry

        lax.fori_loop(low + 1, high, body, 0)

    lanes = lax.broadcasted_iota(jnp.int32, (BLOCKS, 8, 128), 2)
    result = jnp.zeros((BLOCKS, 8, 128), jnp.float32)
    for part in range(2):
        for at in range(2 * SECTIONS):
            total = jnp.sum(sum_ref[part, at], axis=2, keepdims=True)
            result = jnp.where(lanes == LANE_OF_PART[part] + at, total, result)
    out_ref[:, WEIGHT_TILE] = result


WEIGHT_SCRATCH = (2, 2 * SECTIONS, BLOCKS, 8, 128)
IN_VMEM = pl.BlockSpec(memory_space=pltpu.VMEM)


def butterfly_forward(tiles):
    return pl.pallas_call(
        forward_kernel,
        out_shape=jax.ShapeDtypeStruct((BLOCKS, 6, 8, 128), jnp.float32),
        in_specs=[IN_VMEM],
        out_specs=IN_VMEM,
        scratch_shapes=[pltpu.VMEM(WEIGHT_SCRATCH, jnp.float32)],
        compiler_params=pltpu.CompilerParams(vmem_limit_bytes=24 * 1024 * 1024),
        cost_estimate=pl.CostEstimate(flops=4_000_000, bytes_accessed=1_800_000, transcendentals=0),
        name="butterfly_forward",
    )(tiles)


def butterfly_backward(tiles):
    return pl.pallas_call(
        backward_kernel,
        out_shape=jax.ShapeDtypeStruct((BLOCKS, 7, 8, 128), jnp.float32),
        in_specs=[IN_VMEM],
        out_specs=IN_VMEM,
        scratch_shapes=[
            pltpu.VMEM(WEIGHT_SCRATCH, jnp.float32),
            pltpu.VMEM((SECTIONS, BLOCKS, 8, 128), jnp.float32),
            pltpu.VMEM(WEIGHT_SCRATCH, jnp.float32),
        ],
        compiler_params=pltpu.CompilerParams(vmem_limit_bytes=32 * 1024 * 1024),
        cost_estimate=pl.CostEstimate(flops=12_000_000, bytes_accessed=2_600_000, transcendentals=0),
        name="butterfly_backward",
    )(tiles)


def neighbours(low, high):
    count = lax.axis_size("seq")
    before = lax.ppermute(low, "seq", [(i, i + 1) for i in range(count - 1)])
    after = lax.ppermute(high, "seq", [(i + 1, i) for i in range(count - 1)])
    return before, after


def owner_and_tile(group, chunk):
    if group < 16:
        return 2 * group + chunk // 4, chunk % 4
    return 4 * (group - 16) + chunk // 2, 4 + chunk % 2


def split_two(values):
    high = values.astype(jnp.bfloat16)
    return high, (values - high.astype(jnp.float32)).astype(jnp.bfloat16)


def dot_three(left, right, left_dim, right_dim):
    def dot(a, b):
        return lax.dot_general(
            a, b, (((left_dim,), (right_dim,)), ((), ())), preferred_element_type=jnp.float32
        )

    (left_high, left_low), (right_high, right_low) = left, right
    return dot(left_high, right_high) + (dot(left_high, right_low) + dot(left_low, right_high))


def unpack(tile_ref, dest_ref, row):
    for group in range(24):
        for chunk in range(8):
            owner, tile = owner_and_tile(group, chunk)
            dest_ref[row + 8 * group : row + 8 * group + 8, 128 * chunk : 128 * chunk + 128] = (
                tile_ref[owner, tile]
            )


def chunk_of_step(place_ref, step):
    place = place_ref[0]
    return 2 * ((place // 2 + step) % CHIPS) + place % 2


def second_kernel(place_ref, left_a, left_b, right_a, right_b, *refs):
    outs, (right_ref,) = refs[:CHIPS], refs[CHIPS:]
    unpack(right_a, right_ref, 0)
    unpack(right_b, right_ref, 192)
    right = split_two(right_ref[...])
    for step in STEPS:
        rows = pl.ds(pl.multiple_of(chunk_of_step(place_ref, step) * 128, 128), 128)
        left = jnp.concatenate([left_a[:, rows], left_b[:, rows]], axis=0) * WIDTH_SCALE
        outs[step][...] = dot_three(split_two(left), right, 0, 0)


def first_kernel(place_ref, tiles_a, tiles_b, right_a, right_b, *refs):
    outs, (left_ref, tile_ref, right_ref, sem) = refs[:CHIPS], refs[CHIPS:]
    copies = []
    for half, (tiles, right) in enumerate(((tiles_a, right_a), (tiles_b, right_b))):
        copies.append(pltpu.make_async_copy(right, right_ref.at[half], sem.at[2 * half]))
        copies.append(pltpu.make_async_copy(tiles, tile_ref.at[half], sem.at[2 * half + 1]))
    for copy in copies:
        copy.start()
    for half in range(2):
        copies[2 * half].wait()
        right = split_two(right_ref[half])
        copies[2 * half + 1].wait()
        for step in STEPS:
            chunk = chunk_of_step(place_ref, step)
            for group in range(24):
                owner, tile = owner_and_tile(group, chunk)
                left_ref[step, 8 * group : 8 * group + 8, :] = tile_ref[half, owner, tile]
            product = dot_three(split_two(left_ref[step] * WIDTH_SCALE), right, 0, 0)
            if half == 0:
                outs[step][...] = product
            else:
                outs[step][...] += product


def first_products(place, tiles, tiles_other, gated, gated_other):
    piece = jax.ShapeDtypeStruct((128, 1024), jnp.float32)
    return pl.pallas_call(
        first_kernel,
        out_shape=[piece] * CHIPS,
        in_specs=[pl.BlockSpec(memory_space=pltpu.SMEM)] + [IN_HBM] * 4,
        out_specs=[pl.BlockSpec()] * CHIPS,
        scratch_shapes=[
            pltpu.VMEM((CHIPS, 192, 128), jnp.float32),
            pltpu.VMEM((2,) + tiles.shape, jnp.float32),
            pltpu.VMEM((2,) + gated.shape, jnp.float32),
            pltpu.SemaphoreType.DMA((4,)),
        ],
        compiler_params=pltpu.CompilerParams(vmem_limit_bytes=VMEM_LIMIT),
        cost_estimate=pl.CostEstimate(flops=1_200_000_000, bytes_accessed=5_000_000, transcendentals=0),
        name="block_first_products",
    )(place, tiles, tiles_other, gated, gated_other)


def shifted(values, before, after):
    width = values.shape[1]
    lanes = lax.broadcasted_iota(jnp.int32, values.shape, 1)
    prev = jnp.where(lanes == 0, before, pltpu.roll(values, 1, 1))
    return prev, jnp.where(lanes == width - 1, after, pltpu.roll(values, width - 1, 1))


def conv(column_ref, tap, prev, values, later):
    return (
        column_ref[:, tap : tap + 1] * prev
        + column_ref[:, tap + 1 : tap + 2] * values
        + column_ref[:, tap + 2 : tap + 3] * later
    )


def strips(ref, buffer, sem, first, along):
    copies = []
    for at in range(4):
        part = pl.ds(256 * at, 256)
        index = (part, slice(None)) if along == 0 else (slice(None), part)
        copies.append(pltpu.make_async_copy(ref.at[index], buffer.at[index], sem.at[first + at]))
    return copies


IN_HBM = pl.BlockSpec(memory_space=pl.ANY)


def prologue_kernel(
    signal_ref, cot_ref, before_ref, after_ref, taps_q_ref, taps_k_ref, self_ref, partner_ref, first_ref, second_ref,
    packed_ref, gated_ref, mixed_ref, halo_ref, column_ref,
    gated_high, gated_low, mixed_high, mixed_low,
):
    at = pl.program_id(0)

    @pl.when(at == 0)
    def _():
        values = signal_ref[...]
        rows = [taps_q_ref[...], taps_k_ref[...]]
        rows += [ref[section] for ref in (self_ref, partner_ref) for section in range(SECTIONS)]
        rows.append(jnp.zeros((112, values.shape[0]), jnp.float32))
        column_ref[...] = jnp.concatenate(rows, axis=0).T
        before = jnp.broadcast_to(before_ref[...], (128, values.shape[0])).T
        after = jnp.broadcast_to(after_ref[...], (128, values.shape[0])).T
        narrow = lax.broadcasted_iota(jnp.int32, before.shape, 1)
        halo_ref[...] = jnp.where(narrow == 0, before, after)
        prev, later = shifted(values, before[:, :1], after[:, :1])
        gated = conv(column_ref, 3, prev, values, later) * values
        gated_ref[...] = gated
        gated_high[...], gated_low[...] = split_two(gated)
        mixed = cot_ref[...] * conv(column_ref, 0, prev, values, later)
        mixed_ref[...] = mixed
        mixed_high[...], mixed_low[...] = split_two(mixed)
        weights = jnp.concatenate(
            [column_ref[:, 6:16], jnp.zeros((values.shape[0], 118), jnp.float32)], axis=1
        )
        moved = pltpu.roll(weights[128:192], 64, 1)
        for owner in range(BLOCKS):
            low, high = 8 * (owner // 2), 8 * (owner // 4)
            packed_ref[owner, 12] = weights[low : low + 8] + moved[high : high + 8]

    level = dot_three((gated_high[...], gated_low[...]), split_two(first_ref[0]), 1, 1)
    grad = dot_three((mixed_high[...], mixed_low[...]), split_two(second_ref[0]), 1, 0)
    for part in range(COLUMNS // 128):
        chunk = at * (COLUMNS // 128) + part
        for group in range(24):
            owner, tile = owner_and_tile(group, chunk)
            rows, lanes = slice(8 * group, 8 * group + 8), slice(128 * part, 128 * part + 128)
            packed_ref[owner, tile] = level[rows, lanes]
            packed_ref[owner, 6 + tile] = grad[rows, lanes]


def prologue(signal, cotangent, before, after, taps_q, taps_k, mix_self, mix_partner, first, second):
    breadth, height = signal.shape
    whole = lambda shape: pl.BlockSpec(shape, lambda i: (0,) * len(shape))
    full = jax.ShapeDtypeStruct(signal.shape, jnp.float32)
    packed = (BLOCKS, 13, 8, 128)
    return pl.pallas_call(
        prologue_kernel,
        grid=(height // COLUMNS,),
        out_shape=[jax.ShapeDtypeStruct(packed, jnp.float32)]
        + [full] * 2
        + [jax.ShapeDtypeStruct((breadth, 128), jnp.float32)] * 2,
        in_specs=[
            whole(signal.shape),
            whole(signal.shape),
            whole(before.shape),
            whole(after.shape),
            whole(taps_q.shape),
            whole(taps_k.shape),
            whole(mix_self.shape),
            whole(mix_partner.shape),
            pl.BlockSpec((1, COLUMNS, height), lambda i: (0, i, 0)),
            pl.BlockSpec((1, height, COLUMNS), lambda i: (0, 0, i)),
        ],
        out_specs=[whole(packed)] + [whole(signal.shape)] * 2 + [whole((breadth, 128))] * 2,
        scratch_shapes=[pltpu.VMEM(signal.shape, jnp.bfloat16)] * 4,
        compiler_params=pltpu.CompilerParams(vmem_limit_bytes=VMEM_LIMIT),
        cost_estimate=pl.CostEstimate(flops=2_400_000_000, bytes_accessed=15_000_000, transcendentals=0),
        name="prologue",
    )(signal, cotangent, before, after, taps_q, taps_k, mix_self, mix_partner, first, second)


def block_products(kernel, scratch, name, place, *operands):
    piece = jax.ShapeDtypeStruct((128, 1024), jnp.float32)
    return pl.pallas_call(
        kernel,
        out_shape=[piece] * CHIPS,
        in_specs=[pl.BlockSpec(memory_space=pltpu.SMEM)] + [pl.BlockSpec()] * 4,
        out_specs=[pl.BlockSpec()] * CHIPS,
        scratch_shapes=[pltpu.VMEM(scratch, jnp.float32)],
        compiler_params=pltpu.CompilerParams(vmem_limit_bytes=VMEM_LIMIT),
        cost_estimate=pl.CostEstimate(flops=1_200_000_000, bytes_accessed=5_000_000, transcendentals=0),
        name=name,
    )(place, *operands)


def other_core(values):
    return lax.ppermute(values, "ch", [(i, i ^ 1) for i in range(2 * CHIPS)])


def receive_pieces(pieces):
    return [
        lax.ppermute(pieces[step], "ch", [(i, (i + 2 * step) % (2 * CHIPS)) for i in range(2 * CHIPS)])
        for step in STEPS[:-1]
    ]


def tap_products(values, prev, here, later):
    out = []
    for other in (prev, here, later):
        product = values * other
        total = product[:, :128]
        for at in range(128, product.shape[1], 128):
            total = total + product[:, at : at + 128]
        out.append(total)
    return out


def small_columns(sums, first, last, lane):
    lanes = lax.broadcasted_iota(jnp.int32, sums[0].shape, 1)
    total = jnp.zeros(sums[0].shape, jnp.float32)
    for j, value in enumerate(sums):
        total = jnp.where(lanes == lane + j, jnp.sum(value, axis=1, keepdims=True), total)
    total = jnp.where(lanes == lane + 3, first, total)
    return jnp.where(lanes == lane + 4, last, total)


def output_kernel(
    column_ref, halo_ref, tile_hbm, block_hbm, signal_hbm, cot_hbm,
    out_hbm, grad_hbm, small_ref,
    tile_ref, block_ref, signal_ref, cot_ref, level_ref, out_ref, grad_ref, sem,
):
    get_tiles = pltpu.make_async_copy(tile_hbm, tile_ref, sem.at[0])
    get_signal = pltpu.make_async_copy(signal_hbm, signal_ref, sem.at[1])
    get_cot = pltpu.make_async_copy(cot_hbm, cot_ref, sem.at[2])
    get_block = strips(block_hbm.at[0], block_ref, sem, 3, 0)
    get_tiles.start()
    get_signal.start()
    get_block[0].start()
    get_cot.start()
    for copy in get_block[1:]:
        copy.start()
    get_tiles.wait()
    unpack(tile_ref, level_ref, 0)
    left = split_two(level_ref[...])
    get_signal.wait()
    values = signal_ref[...]
    prev, later = shifted(values, halo_ref[:, 0:1], halo_ref[:, 1:2])
    query = conv(column_ref, 0, prev, values, later)
    sums, puts = None, []
    for at in range(4):
        part = slice(256 * at, 256 * at + 256)
        get_block[at].wait()
        mixed = dot_three(left, split_two(block_ref[part, :]), 1, 1)
        if at == 0:
            get_cot.wait()
        out_ref[:, part] = query[:, part] * mixed
        grad = cot_ref[:, part] * mixed
        grad_ref[:, part] = grad
        put = pltpu.make_async_copy(out_ref.at[:, part], out_hbm.at[:, part], sem.at[7 + at])
        put.start()
        puts.append(put)
        new = tap_products(grad, prev[:, part], values[:, part], later[:, part])
        sums = new if sums is None else [a + b for a, b in zip(sums, new)]
    small_ref[...] = small_columns(sums, grad_ref[:, 0:1], grad_ref[:, 1023:1024], 0)
    rows = grad_ref[...]
    behind, ahead = shifted(rows, 0.0, 0.0)
    level_ref[...] = conv(column_ref, 0, ahead, rows, behind)
    put = pltpu.make_async_copy(level_ref, grad_hbm, sem.at[11])
    put.start()
    puts.append(put)
    for put in puts:
        put.wait()


def make_output(tiles, block, cotangent, signal, columns, halo):
    full = jax.ShapeDtypeStruct(signal.shape, jnp.float32)
    buffer = pltpu.VMEM(signal.shape, jnp.float32)
    return pl.pallas_call(
        output_kernel,
        out_shape=[full, full, jax.ShapeDtypeStruct((signal.shape[0], 128), jnp.float32)],
        in_specs=[pl.BlockSpec()] * 2 + [IN_HBM] * 4,
        out_specs=[IN_HBM] * 2 + [pl.BlockSpec()],
        scratch_shapes=[
            pltpu.VMEM(tiles.shape, jnp.float32),
            pltpu.VMEM(block.shape[1:], jnp.float32),
            buffer,
            buffer,
            buffer,
            buffer,
            buffer,
            pltpu.SemaphoreType.DMA((12,)),
        ],
        compiler_params=pltpu.CompilerParams(vmem_limit_bytes=VMEM_LIMIT),
        cost_estimate=pl.CostEstimate(flops=1_200_000_000, bytes_accessed=9_000_000, transcendentals=0),
        name="make_output",
    )(columns, halo, tiles, block, signal, cotangent)


def tap_kernel(halo_ref, signal_ref, block_ref, out_ref, ends_ref, edge_ref, high_ref, low_ref):
    at = pl.program_id(0)
    breadth = signal_ref.shape[0]

    @pl.when(at == 0)
    def _():
        values = signal_ref[...]
        prev, later = shifted(values, halo_ref[:, 0:1], halo_ref[:, 1:2])
        for j, other in enumerate((prev, values, later)):
            rows = slice(breadth * j, breadth * j + breadth)
            high_ref[rows, :], low_ref[rows, :] = split_two(values * other)
        lanes = lax.broadcasted_iota(jnp.int32, (breadth, 128), 1)
        ends_ref[...] = jnp.where(lanes == 0, values[:, :1], values[:, 1023:1024])

    block = block_ref[0]
    out_ref[...] = dot_three((high_ref[...], low_ref[...]), split_two(block), 1, 1)
    first = block[:, 0:128].T
    last = block[:, 896:1024].T
    edge_ref[0:8, :] = jnp.broadcast_to(first[0:1], (8, first.shape[1]))
    edge_ref[8:16, :] = jnp.broadcast_to(last[127:128], (8, first.shape[1]))


def tap_weights(signal, halo, block):
    breadth, height = signal.shape
    whole = lambda shape: pl.BlockSpec(shape, lambda i: (0,) * len(shape))
    return pl.pallas_call(
        tap_kernel,
        grid=(height // COLUMNS,),
        out_shape=[
            jax.ShapeDtypeStruct((3 * breadth, height), jnp.float32),
            jax.ShapeDtypeStruct((breadth, 128), jnp.float32),
            jax.ShapeDtypeStruct((16, height), jnp.float32),
        ],
        in_specs=[
            whole(halo.shape),
            whole(signal.shape),
            pl.BlockSpec((1, COLUMNS, height), lambda i: (0, i, 0)),
        ],
        out_specs=[
            pl.BlockSpec((3 * breadth, COLUMNS), lambda i: (0, i)),
            whole((breadth, 128)),
            pl.BlockSpec((16, COLUMNS), lambda i: (0, i)),
        ],
        scratch_shapes=[pltpu.VMEM((3 * breadth, height), jnp.bfloat16)] * 2,
        compiler_params=pltpu.CompilerParams(vmem_limit_bytes=VMEM_LIMIT),
        cost_estimate=pl.CostEstimate(flops=3_600_000_000, bytes_accessed=8_000_000, transcendentals=0),
        name="tap_weights",
    )(halo, signal, block)


def send_kernel(tile_ref, weight_ref, ends_ref, edge_ref, small_in_ref, send_ref):
    breadth = ends_ref.shape[0]
    totals = [[] for _ in range(5)]
    for group in range(24):
        sums = [None] * 5
        for chunk in range(8):
            owner, tile = owner_and_tile(group, chunk)
            values = tile_ref[owner, tile]
            lanes = slice(128 * chunk, 128 * chunk + 128)
            others = [
                weight_ref[breadth * j + 8 * group : breadth * j + 8 * group + 8, lanes] for j in range(3)
            ] + [edge_ref[0:8, lanes], edge_ref[8:16, lanes]]
            for j, other in enumerate(others):
                product = values * other
                sums[j] = product if sums[j] is None else sums[j] + product
        for j in range(5):
            totals[j].append(sums[j])
    lanes = lax.broadcasted_iota(jnp.int32, (breadth, 128), 1)
    small = small_in_ref[...]
    for j in range(5):
        total = jnp.sum(jnp.concatenate(totals[j], axis=0), axis=1, keepdims=True)
        if j >= 3:
            total = total * ends_ref[:, j - 3 : j - 2]
        small = small + jnp.where(lanes == 5 + j, total, 0.0)
    rows = small.T
    tail = jnp.concatenate([rows[0:5, 128:192], rows[5:10, 128:192]], axis=1)
    packed = jnp.concatenate([rows[0:10, 0:128], tail, jnp.zeros((1, 128), jnp.float32)], axis=0)
    for block in range(BLOCKS):
        send_ref[block] = packed


def make_send(tiles, weights, ends, edges, small):
    return pl.pallas_call(
        send_kernel,
        out_shape=jax.ShapeDtypeStruct((BLOCKS, 16, 128), jnp.float32),
        in_specs=[pl.BlockSpec()] * 5,
        out_specs=pl.BlockSpec(),
        compiler_params=pltpu.CompilerParams(vmem_limit_bytes=VMEM_LIMIT),
        cost_estimate=pl.CostEstimate(flops=2_000_000, bytes_accessed=4_000_000, transcendentals=0),
        name="make_send",
    )(tiles, weights, ends, edges, small)


def inside_kernel(
    halo_ref, column_ref, tile_hbm, block_hbm, signal_hbm, query_hbm,
    out_hbm, self_ref, partner_ref,
    tile_ref, block_ref, signal_ref, query_ref, level_ref, gated_ref, sem,
):
    get_tiles = pltpu.make_async_copy(tile_hbm, tile_ref, sem.at[0])
    get_signal = pltpu.make_async_copy(signal_hbm, signal_ref, sem.at[1])
    get_query = pltpu.make_async_copy(query_hbm, query_ref, sem.at[2])
    get_block = strips(block_hbm.at[0], block_ref, sem, 3, 1)
    get_tiles.start()
    for copy in get_block:
        copy.start()
    get_signal.start()
    get_query.start()
    get_tiles.wait()
    unpack(tile_ref, level_ref, 0)
    left = split_two(level_ref[...])
    for at in range(4):
        part = slice(256 * at, 256 * at + 256)
        get_block[at].wait()
        gated_ref[:, part] = dot_three(left, split_two(block_ref[:, part]), 1, 0)
    get_signal.wait()
    get_query.wait()
    values, gated = signal_ref[...], gated_ref[...]
    prev, later = shifted(values, halo_ref[:, 0:1], halo_ref[:, 1:2])
    total = gated * conv(column_ref, 3, prev, values, later)
    rows = gated * values
    behind, ahead = shifted(rows, 0.0, 0.0)
    total = total + query_ref[...] + conv(column_ref, 3, ahead, rows, behind)
    level_ref[...] = total
    put = pltpu.make_async_copy(level_ref, out_hbm, sem.at[7])
    put.start()
    mix_ref = tile_ref.at[:, WEIGHT_TILE]
    mixes = []
    for group in range(16):
        mixes.append(mix_ref[2 * group] + mix_ref[2 * group + 1])
    for group in range(8):
        four = mix_ref[4 * group] + mix_ref[4 * group + 1] + mix_ref[4 * group + 2] + mix_ref[4 * group + 3]
        mixes.append(pltpu.roll(four, 64, 1))
    mixes = (jnp.concatenate(mixes, axis=0) * ROW_SCALE).T
    for section in range(SECTIONS):
        self_ref[section] = mixes[section : section + 1]
        partner_ref[section] = mixes[SECTIONS + section : SECTIONS + section + 1]
    put.wait()


def make_inside(tiles, block, signal, grad_query, halo, columns):
    mix = jax.ShapeDtypeStruct((SECTIONS, 1, signal.shape[0]), jnp.float32)
    buffer = pltpu.VMEM(signal.shape, jnp.float32)
    return pl.pallas_call(
        inside_kernel,
        out_shape=[jax.ShapeDtypeStruct(signal.shape, jnp.float32), mix, mix],
        in_specs=[pl.BlockSpec()] * 2 + [IN_HBM] * 4,
        out_specs=[IN_HBM] + [pl.BlockSpec()] * 2,
        scratch_shapes=[
            pltpu.VMEM(tiles.shape, jnp.float32),
            pltpu.VMEM(block.shape[1:], jnp.float32),
            buffer,
            buffer,
            buffer,
            buffer,
            pltpu.SemaphoreType.DMA((8,)),
        ],
        compiler_params=pltpu.CompilerParams(vmem_limit_bytes=VMEM_LIMIT),
        cost_estimate=pl.CostEstimate(flops=1_200_000_000, bytes_accessed=8_000_000, transcendentals=0),
        name="make_inside",
    )(halo, columns, tiles, block, signal, grad_query)


def edge_kernel(block_ref, got_ref, column_ref, in_ref, out_ref, tap_q_ref, tap_k_ref):
    at = pl.program_id(0)
    block = block_ref[0]

    def table(packed):
        low = packed[0:10]
        high = jnp.concatenate([packed[10:15, 0:64], packed[10:15, 64:128]], axis=0)
        return jnp.concatenate([low, high], axis=1)

    def columns(packed):
        rows = table(packed)
        return jnp.concatenate([rows, jnp.zeros((118, 192), jnp.float32)], axis=0).T

    source = jnp.where(at == 0, jnp.maximum(block - 1, 0), jnp.minimum(block + 1, BLOCKS - 1))
    inside = jnp.where(at == 0, block > 0, block < BLOCKS - 1)
    halo = jnp.where(inside, columns(got_ref[source]), 0.0)
    lanes = lax.broadcasted_iota(jnp.int32, (192, 128), 1)

    @pl.when(at == 0)
    def _():
        extra = column_ref[:, 2:3] * halo[:, 4:5] + column_ref[:, 5:6] * halo[:, 9:10]
        out_ref[...] = in_ref[...] + jnp.where(lanes == 0, extra, 0.0)
        sums = table(jnp.sum(got_ref[...], axis=0)) * TOKEN_SCALE
        tap_q_ref[...] = sums[0:3]
        tap_k_ref[...] = sums[5:8]

    @pl.when(at == 1)
    def _():
        extra = column_ref[:, 0:1] * halo[:, 3:4] + column_ref[:, 3:4] * halo[:, 8:9]
        out_ref[...] = in_ref[...] + jnp.where(lanes == 127, extra, 0.0)


def make_edges(block, got, columns, inside):
    whole = lambda shape: pl.BlockSpec(shape, lambda i: (0,) * len(shape))
    last = inside.shape[1] // 128 - 1
    strip = pl.BlockSpec((inside.shape[0], 128), lambda i: (0, last * i))
    return pl.pallas_call(
        edge_kernel,
        grid=(2,),
        out_shape=[
            jax.ShapeDtypeStruct(inside.shape, jnp.float32),
            jax.ShapeDtypeStruct((3, inside.shape[0]), jnp.float32),
            jax.ShapeDtypeStruct((3, inside.shape[0]), jnp.float32),
        ],
        in_specs=[
            pl.BlockSpec(memory_space=pltpu.SMEM),
            whole(got.shape),
            whole(columns.shape),
            strip,
        ],
        out_specs=[strip] + [whole((3, inside.shape[0]))] * 2,
        input_output_aliases={3: 0},
        compiler_params=pltpu.CompilerParams(vmem_limit_bytes=VMEM_LIMIT),
        cost_estimate=pl.CostEstimate(flops=200_000, bytes_accessed=900_000, transcendentals=0),
        name="make_edges",
    )(block, got, columns, inside)


def local(signal, cotangent, kernel_q, kernel_k, block_first, block_second, mix_self, mix_partner):
    before, after = neighbours(signal[-1:], signal[:1])
    signal, cotangent = signal.T, cotangent.T
    swap = lambda tiles: lax.all_to_all(tiles, "seq", 0, 0, tiled=True)
    after_both = lax.optimization_barrier
    place = lax.axis_index("ch").reshape(1)
    block = lax.axis_index("seq").reshape(1)

    packed, gated_in, grad_mixed, halo, columns = prologue(
        signal, cotangent, before, after, kernel_q, kernel_k, mix_self, mix_partner,
        block_first, block_second,
    )
    incoming = swap(packed)
    gated_other, mixed_other = other_core(gated_in), other_core(grad_mixed)
    level_last = swap(butterfly_forward(incoming))
    grad_tiles = butterfly_backward(incoming)
    tap_parts = tap_weights(signal, halo, block_first)
    level_last, grad_tiles, tap_parts, gated_other, mixed_other = after_both(
        (level_last, grad_tiles, tap_parts, gated_other, mixed_other)
    )
    returned = swap(grad_tiles)

    level_other = other_core(level_last)
    pieces = block_products(
        second_kernel, (384, 1024), "block_second_products", place,
        grad_mixed, mixed_other, level_last, level_other,
    )
    level_last, pieces = after_both((level_last, pieces))
    output, grad_query, small = make_output(
        level_last, block_second, cotangent, signal, columns, halo
    )
    second_received = receive_pieces(pieces)
    second_own = pieces[0]
    returned, small, second_received[1:] = after_both((returned, small, second_received[1:]))

    returned_other = other_core(returned)
    send = make_send(returned, *tap_parts, small)
    returned_other, send = after_both((returned_other, send))
    pieces = first_products(place, returned, returned_other, gated_in, gated_other)
    first_received = receive_pieces(pieces)
    send, pieces = after_both((send, pieces))
    got = swap(send)
    inside, mix_self_grad, mix_partner_grad = make_inside(
        returned, block_first, signal, grad_query, halo, columns
    )
    grad_second = second_own + second_received[0] + second_received[1] + second_received[2]
    grad_signal, tap_q_grad, tap_k_grad = make_edges(block, got, columns, inside)
    grad_first = pieces[0] + first_received[0] + first_received[1] + first_received[2]

    return (
        output.T,
        grad_signal.T,
        tap_q_grad,
        tap_k_grad,
        grad_first[None],
        grad_second[None],
        mix_self_grad,
        mix_partner_grad,
    )


def solution(mesh):
    return jax.shard_map(
        local,
        mesh=mesh,
        in_specs=(
            P("seq", "ch"),
            P("seq", "ch"),
            P(None, "ch"),
            P(None, "ch"),
            P("seq", None, None),
            P("seq", None, None),
            P(None, "seq", "ch"),
            P(None, "seq", "ch"),
        ),
        out_specs=(
            P("seq", "ch"),
            P("seq", "ch"),
            P(None, "ch"),
            P(None, "ch"),
            P("seq", "ch", None),
            P("seq", "ch", None),
            P(None, "seq", "ch"),
            P(None, "seq", "ch"),
        ),
        check_vma=False,
    )
```

```python
import math

import jax
import jax.numpy as jnp
from jax import lax
from jax.experimental import pallas as pl
from jax.experimental.pallas import tpu as pltpu
from jax.sharding import PartitionSpec as P

D = 1536
SECTIONS = 5
BLOCKS = 32
PARTS = ((0, 4), (4, 6))
LANE_OF_PART = (0, 64)
WEIGHT_TILE = 6
CHIPS = 4
STEPS = (2, 1, 3, 0)
COLUMNS = 256
VMEM_LIMIT = 56 * 1024 * 1024
WIDTH_SCALE = 1.0 / math.sqrt(D)
ROW_SCALE = 1.0 / math.sqrt(1024)
TOKEN_SCALE = 1.0 / math.sqrt(32768)

def flip(values, section):
    stride = 2**section
    pieces = []
    for at in range(0, BLOCKS, 2 * stride):
        pieces.append(values[at + stride : at + 2 * stride])
        pieces.append(values[at : at + stride])
    return jnp.concatenate(pieces, axis=0)


def load_weights(in_ref, weight_ref):
    for part in range(2):
        for at in range(2 * SECTIONS):
            lane = LANE_OF_PART[part] + at
            column = in_ref[:, 12, :, lane : lane + 1]
            weight_ref[part, at] = jnp.broadcast_to(column, (BLOCKS, 8, 128))


def step_forward(level, weight_ref, part, section):
    return (
        weight_ref[part, section] * level
        + weight_ref[part, SECTIONS + section] * flip(level, section)
    )


def forward_kernel(in_ref, out_ref, weight_ref):
    load_weights(in_ref, weight_ref)
    for part, (low, high) in enumerate(PARTS):

        def one_tile(tile, carry):
            level = in_ref[:, tile]
            for section in range(SECTIONS):
                level = step_forward(level, weight_ref, part, section)
            out_ref[:, tile] = level
            return carry

        lax.fori_loop(low, high, one_tile, 0)


def backward_kernel(in_ref, out_ref, weight_ref, level_ref, sum_ref):
    load_weights(in_ref, weight_ref)
    for part, (low, high) in enumerate(PARTS):

        def one_tile(tile, first):
            level = in_ref[:, tile]
            for section in range(SECTIONS):
                level_ref[section] = level
                if section < SECTIONS - 1:
                    level = step_forward(level, weight_ref, part, section)
            grad = in_ref[:, 6 + tile]
            for section in reversed(range(SECTIONS)):
                level = level_ref[section]
                own = grad * level
                other = grad * flip(level, section)
                if first:
                    sum_ref[part, section] = own
                    sum_ref[part, SECTIONS + section] = other
                else:
                    sum_ref[part, section] += own
                    sum_ref[part, SECTIONS + section] += other
                grad = weight_ref[part, section] * grad + flip(
                    weight_ref[part, SECTIONS + section] * grad, section
                )
            out_ref[:, tile] = grad

        one_tile(low, True)

        def body(tile, carry):
            one_tile(tile, False)
            return carry

        lax.fori_loop(low + 1, high, body, 0)

    lanes = lax.broadcasted_iota(jnp.int32, (BLOCKS, 8, 128), 2)
    result = jnp.zeros((BLOCKS, 8, 128), jnp.float32)
    for part in range(2):
        for at in range(2 * SECTIONS):
            total = jnp.sum(sum_ref[part, at], axis=2, keepdims=True)
            result = jnp.where(lanes == LANE_OF_PART[part] + at, total, result)
    out_ref[:, WEIGHT_TILE] = result


WEIGHT_SCRATCH = (2, 2 * SECTIONS, BLOCKS, 8, 128)
IN_VMEM = pl.BlockSpec(memory_space=pltpu.VMEM)


def butterfly_forward(tiles):
    return pl.pallas_call(
        forward_kernel,
        out_shape=jax.ShapeDtypeStruct((BLOCKS, 6, 8, 128), jnp.float32),
        in_specs=[IN_VMEM],
        out_specs=IN_VMEM,
        scratch_shapes=[pltpu.VMEM(WEIGHT_SCRATCH, jnp.float32)],
        compiler_params=pltpu.CompilerParams(vmem_limit_bytes=24 * 1024 * 1024),
        cost_estimate=pl.CostEstimate(flops=4_000_000, bytes_accessed=1_800_000, transcendentals=0),
        name="butterfly_forward",
    )(tiles)


def butterfly_backward(tiles):
    return pl.pallas_call(
        backward_kernel,
        out_shape=jax.ShapeDtypeStruct((BLOCKS, 7, 8, 128), jnp.float32),
        in_specs=[IN_VMEM],
        out_specs=IN_VMEM,
        scratch_shapes=[
            pltpu.VMEM(WEIGHT_SCRATCH, jnp.float32),
            pltpu.VMEM((SECTIONS, BLOCKS, 8, 128), jnp.float32),
            pltpu.VMEM(WEIGHT_SCRATCH, jnp.float32),
        ],
        compiler_params=pltpu.CompilerParams(vmem_limit_bytes=32 * 1024 * 1024),
        cost_estimate=pl.CostEstimate(flops=12_000_000, bytes_accessed=2_600_000, transcendentals=0),
        name="butterfly_backward",
    )(tiles)


def neighbours(low, high):
    count = lax.axis_size("seq")
    before = lax.ppermute(low, "seq", [(i, i + 1) for i in range(count - 1)])
    after = lax.ppermute(high, "seq", [(i + 1, i) for i in range(count - 1)])
    return before, after


def owner_and_tile(group, chunk):
    if group < 16:
        return 2 * group + chunk // 4, chunk % 4
    return 4 * (group - 16) + chunk // 2, 4 + chunk % 2


def split_two(values):
    high = values.astype(jnp.bfloat16)
    return high, (values - high.astype(jnp.float32)).astype(jnp.bfloat16)


def dot_three(left, right, left_dim, right_dim):
    def dot(a, b):
        return lax.dot_general(
            a, b, (((left_dim,), (right_dim,)), ((), ())), preferred_element_type=jnp.float32
        )

    (left_high, left_low), (right_high, right_low) = left, right
    return dot(left_high, right_high) + (dot(left_high, right_low) + dot(left_low, right_high))


def unpack(tile_ref, dest_ref, row):
    for group in range(24):
        for chunk in range(8):
            owner, tile = owner_and_tile(group, chunk)
            dest_ref[row + 8 * group : row + 8 * group + 8, 128 * chunk : 128 * chunk + 128] = (
                tile_ref[owner, tile]
            )


def chunk_of_step(place_ref, step):
    place = place_ref[0]
    return 2 * ((place // 2 + step) % CHIPS) + place % 2


def second_kernel(place_ref, left_a, left_b, right_a, right_b, *refs):
    outs, (right_ref,) = refs[:CHIPS], refs[CHIPS:]
    unpack(right_a, right_ref, 0)
    unpack(right_b, right_ref, 192)
    right = split_two(right_ref[...])
    for step in STEPS:
        rows = pl.ds(pl.multiple_of(chunk_of_step(place_ref, step) * 128, 128), 128)
        left = jnp.concatenate([left_a[:, rows], left_b[:, rows]], axis=0) * WIDTH_SCALE
        outs[step][...] = dot_three(split_two(left), right, 0, 0)


def first_kernel(place_ref, tiles_a, tiles_b, right_a, right_b, *refs):
    outs, (left_ref, tile_ref, right_ref, total_ref, sem) = refs[:CHIPS], refs[CHIPS:]
    puts = []
    copies = []
    for half, (tiles, right) in enumerate(((tiles_a, right_a), (tiles_b, right_b))):
        copies.append(pltpu.make_async_copy(right, right_ref.at[half], sem.at[2 * half]))
        copies.append(pltpu.make_async_copy(tiles, tile_ref.at[half], sem.at[2 * half + 1]))
    for copy in copies:
        copy.start()
    for half in range(2):
        copies[2 * half].wait()
        right = split_two(right_ref[half])
        copies[2 * half + 1].wait()
        for step in STEPS:
            chunk = chunk_of_step(place_ref, step)
            for group in range(24):
                owner, tile = owner_and_tile(group, chunk)
                left_ref[step, 8 * group : 8 * group + 8, :] = tile_ref[half, owner, tile]
            product = dot_three(split_two(left_ref[step] * WIDTH_SCALE), right, 0, 0)
            if half == 0:
                total_ref[step] = product
            else:
                total_ref[step] += product
                puts.append(pltpu.make_async_copy(total_ref.at[step], outs[step], sem.at[4 + step]))
                puts[-1].start()
    for put in puts:
        put.wait()


def first_products(place, tiles, tiles_other, gated, gated_other):
    piece = jax.ShapeDtypeStruct((128, 1024), jnp.float32)
    return pl.pallas_call(
        first_kernel,
        out_shape=[piece] * CHIPS,
        in_specs=[pl.BlockSpec(memory_space=pltpu.SMEM)] + [IN_HBM] * 4,
        out_specs=[IN_HBM] * CHIPS,
        scratch_shapes=[
            pltpu.VMEM((CHIPS, 192, 128), jnp.float32),
            pltpu.VMEM((2,) + tiles.shape, jnp.float32),
            pltpu.VMEM((2,) + gated.shape, jnp.float32),
            pltpu.VMEM((CHIPS, 128, 1024), jnp.float32),
            pltpu.SemaphoreType.DMA((8,)),
        ],
        compiler_params=pltpu.CompilerParams(vmem_limit_bytes=VMEM_LIMIT),
        cost_estimate=pl.CostEstimate(flops=1_200_000_000, bytes_accessed=5_000_000, transcendentals=0),
        name="block_first_products",
    )(place, tiles, tiles_other, gated, gated_other)


def shifted(values, before, after):
    width = values.shape[1]
    lanes = lax.broadcasted_iota(jnp.int32, values.shape, 1)
    prev = jnp.where(lanes == 0, before, pltpu.roll(values, 1, 1))
    return prev, jnp.where(lanes == width - 1, after, pltpu.roll(values, width - 1, 1))


def conv(column_ref, tap, prev, values, later):
    return (
        column_ref[:, tap : tap + 1] * prev
        + column_ref[:, tap + 1 : tap + 2] * values
        + column_ref[:, tap + 2 : tap + 3] * later
    )


def strips(ref, buffer, sem, first, along):
    copies = []
    for at in range(4):
        part = pl.ds(256 * at, 256)
        index = (part, slice(None)) if along == 0 else (slice(None), part)
        copies.append(pltpu.make_async_copy(ref.at[index], buffer.at[index], sem.at[first + at]))
    return copies


IN_HBM = pl.BlockSpec(memory_space=pl.ANY)


def prologue_kernel(
    signal_ref, cot_ref, before_ref, after_ref, taps_q_ref, taps_k_ref, self_ref, partner_ref, first_ref, second_ref,
    packed_ref, gated_ref, mixed_ref, halo_ref, column_ref,
    gated_high, gated_low, mixed_high, mixed_low,
):
    at = pl.program_id(0)

    @pl.when(at == 0)
    def _():
        values = signal_ref[...]
        rows = [taps_q_ref[...], taps_k_ref[...]]
        rows += [ref[section] for ref in (self_ref, partner_ref) for section in range(SECTIONS)]
        rows.append(jnp.zeros((112, values.shape[0]), jnp.float32))
        column_ref[...] = jnp.concatenate(rows, axis=0).T
        before = jnp.broadcast_to(before_ref[...], (128, values.shape[0])).T
        after = jnp.broadcast_to(after_ref[...], (128, values.shape[0])).T
        narrow = lax.broadcasted_iota(jnp.int32, before.shape, 1)
        halo_ref[...] = jnp.where(narrow == 0, before, after)
        prev, later = shifted(values, before[:, :1], after[:, :1])
        gated = conv(column_ref, 3, prev, values, later) * values
        gated_ref[...] = gated
        gated_high[...], gated_low[...] = split_two(gated)
        mixed = cot_ref[...] * conv(column_ref, 0, prev, values, later)
        mixed_ref[...] = mixed
        mixed_high[...], mixed_low[...] = split_two(mixed)
        weights = jnp.concatenate(
            [column_ref[:, 6:16], jnp.zeros((values.shape[0], 118), jnp.float32)], axis=1
        )
        moved = pltpu.roll(weights[128:192], 64, 1)
        for owner in range(BLOCKS):
            low, high = 8 * (owner // 2), 8 * (owner // 4)
            packed_ref[owner, 12] = weights[low : low + 8] + moved[high : high + 8]

    level = dot_three((gated_high[...], gated_low[...]), split_two(first_ref[0]), 1, 1)
    grad = dot_three((mixed_high[...], mixed_low[...]), split_two(second_ref[0]), 1, 0)
    for part in range(COLUMNS // 128):
        chunk = at * (COLUMNS // 128) + part
        for group in range(24):
            owner, tile = owner_and_tile(group, chunk)
            rows, lanes = slice(8 * group, 8 * group + 8), slice(128 * part, 128 * part + 128)
            packed_ref[owner, tile] = level[rows, lanes]
            packed_ref[owner, 6 + tile] = grad[rows, lanes]


def prologue(signal, cotangent, before, after, taps_q, taps_k, mix_self, mix_partner, first, second):
    breadth, height = signal.shape
    whole = lambda shape: pl.BlockSpec(shape, lambda i: (0,) * len(shape))
    full = jax.ShapeDtypeStruct(signal.shape, jnp.float32)
    packed = (BLOCKS, 13, 8, 128)
    return pl.pallas_call(
        prologue_kernel,
        grid=(height // COLUMNS,),
        out_shape=[jax.ShapeDtypeStruct(packed, jnp.float32)]
        + [full] * 2
        + [jax.ShapeDtypeStruct((breadth, 128), jnp.float32)] * 2,
        in_specs=[
            whole(signal.shape),
            whole(signal.shape),
            whole(before.shape),
            whole(after.shape),
            whole(taps_q.shape),
            whole(taps_k.shape),
            whole(mix_self.shape),
            whole(mix_partner.shape),
            pl.BlockSpec((1, COLUMNS, height), lambda i: (0, i, 0)),
            pl.BlockSpec((1, height, COLUMNS), lambda i: (0, 0, i)),
        ],
        out_specs=[whole(packed)] + [whole(signal.shape)] * 2 + [whole((breadth, 128))] * 2,
        scratch_shapes=[pltpu.VMEM(signal.shape, jnp.bfloat16)] * 4,
        compiler_params=pltpu.CompilerParams(vmem_limit_bytes=VMEM_LIMIT),
        cost_estimate=pl.CostEstimate(flops=2_400_000_000, bytes_accessed=15_000_000, transcendentals=0),
        name="prologue",
    )(signal, cotangent, before, after, taps_q, taps_k, mix_self, mix_partner, first, second)


def block_products(kernel, scratch, name, place, *operands):
    piece = jax.ShapeDtypeStruct((128, 1024), jnp.float32)
    return pl.pallas_call(
        kernel,
        out_shape=[piece] * CHIPS,
        in_specs=[pl.BlockSpec(memory_space=pltpu.SMEM)] + [pl.BlockSpec()] * 4,
        out_specs=[pl.BlockSpec()] * CHIPS,
        scratch_shapes=[pltpu.VMEM(scratch, jnp.float32)],
        compiler_params=pltpu.CompilerParams(vmem_limit_bytes=VMEM_LIMIT),
        cost_estimate=pl.CostEstimate(flops=1_200_000_000, bytes_accessed=5_000_000, transcendentals=0),
        name=name,
    )(place, *operands)


def other_core(values):
    return lax.ppermute(values, "ch", [(i, i ^ 1) for i in range(2 * CHIPS)])


def receive_pieces(pieces):
    return [
        lax.ppermute(pieces[step], "ch", [(i, (i + 2 * step) % (2 * CHIPS)) for i in range(2 * CHIPS)])
        for step in STEPS[:-1]
    ]


def tap_products(values, prev, here, later):
    out = []
    for other in (prev, here, later):
        product = values * other
        total = product[:, :128]
        for at in range(128, product.shape[1], 128):
            total = total + product[:, at : at + 128]
        out.append(total)
    return out


def small_columns(sums, first, last, lane):
    lanes = lax.broadcasted_iota(jnp.int32, sums[0].shape, 1)
    total = jnp.zeros(sums[0].shape, jnp.float32)
    for j, value in enumerate(sums):
        total = jnp.where(lanes == lane + j, jnp.sum(value, axis=1, keepdims=True), total)
    total = jnp.where(lanes == lane + 3, first, total)
    return jnp.where(lanes == lane + 4, last, total)


def output_kernel(
    column_ref, halo_ref, tile_hbm, block_hbm, signal_hbm, cot_hbm,
    out_hbm, grad_hbm, small_ref,
    tile_ref, block_ref, signal_ref, cot_ref, level_ref, out_ref, grad_ref, sem,
):
    get_tiles = pltpu.make_async_copy(tile_hbm, tile_ref, sem.at[0])
    get_signal = pltpu.make_async_copy(signal_hbm, signal_ref, sem.at[1])
    get_cot = pltpu.make_async_copy(cot_hbm, cot_ref, sem.at[2])
    get_block = strips(block_hbm.at[0], block_ref, sem, 3, 0)
    get_tiles.start()
    get_signal.start()
    get_block[0].start()
    get_cot.start()
    for copy in get_block[1:]:
        copy.start()
    get_tiles.wait()
    unpack(tile_ref, level_ref, 0)
    left = split_two(level_ref[...])
    get_signal.wait()
    values = signal_ref[...]
    prev, later = shifted(values, halo_ref[:, 0:1], halo_ref[:, 1:2])
    query = conv(column_ref, 0, prev, values, later)
    sums, puts = None, []
    for at in range(4):
        part = slice(256 * at, 256 * at + 256)
        get_block[at].wait()
        mixed = dot_three(left, split_two(block_ref[part, :]), 1, 1)
        if at == 0:
            get_cot.wait()
        out_ref[:, part] = query[:, part] * mixed
        grad = cot_ref[:, part] * mixed
        grad_ref[:, part] = grad
        put = pltpu.make_async_copy(out_ref.at[:, part], out_hbm.at[:, part], sem.at[7 + at])
        put.start()
        puts.append(put)
        new = tap_products(grad, prev[:, part], values[:, part], later[:, part])
        sums = new if sums is None else [a + b for a, b in zip(sums, new)]
    small_ref[...] = small_columns(sums, grad_ref[:, 0:1], grad_ref[:, 1023:1024], 0)
    rows = grad_ref[...]
    behind, ahead = shifted(rows, 0.0, 0.0)
    level_ref[...] = conv(column_ref, 0, ahead, rows, behind)
    put = pltpu.make_async_copy(level_ref, grad_hbm, sem.at[11])
    put.start()
    puts.append(put)
    for put in puts:
        put.wait()


def make_output(tiles, block, cotangent, signal, columns, halo):
    full = jax.ShapeDtypeStruct(signal.shape, jnp.float32)
    buffer = pltpu.VMEM(signal.shape, jnp.float32)
    return pl.pallas_call(
        output_kernel,
        out_shape=[full, full, jax.ShapeDtypeStruct((signal.shape[0], 128), jnp.float32)],
        in_specs=[pl.BlockSpec()] * 2 + [IN_HBM] * 4,
        out_specs=[IN_HBM] * 2 + [pl.BlockSpec()],
        scratch_shapes=[
            pltpu.VMEM(tiles.shape, jnp.float32),
            pltpu.VMEM(block.shape[1:], jnp.float32),
            buffer,
            buffer,
            buffer,
            buffer,
            buffer,
            pltpu.SemaphoreType.DMA((12,)),
        ],
        compiler_params=pltpu.CompilerParams(vmem_limit_bytes=VMEM_LIMIT),
        cost_estimate=pl.CostEstimate(flops=1_200_000_000, bytes_accessed=9_000_000, transcendentals=0),
        name="make_output",
    )(columns, halo, tiles, block, signal, cotangent)


def tap_kernel(halo_ref, signal_ref, block_ref, out_ref, ends_ref, edge_ref, high_ref, low_ref):
    at = pl.program_id(0)
    breadth = signal_ref.shape[0]

    @pl.when(at == 0)
    def _():
        values = signal_ref[...]
        prev, later = shifted(values, halo_ref[:, 0:1], halo_ref[:, 1:2])
        for j, other in enumerate((prev, values, later)):
            rows = slice(breadth * j, breadth * j + breadth)
            high_ref[rows, :], low_ref[rows, :] = split_two(values * other)
        lanes = lax.broadcasted_iota(jnp.int32, (breadth, 128), 1)
        ends_ref[...] = jnp.where(lanes == 0, values[:, :1], values[:, 1023:1024])

    block = block_ref[0]
    out_ref[...] = dot_three((high_ref[...], low_ref[...]), split_two(block), 1, 1)
    first = block[:, 0:128].T
    last = block[:, 896:1024].T
    edge_ref[0:8, :] = jnp.broadcast_to(first[0:1], (8, first.shape[1]))
    edge_ref[8:16, :] = jnp.broadcast_to(last[127:128], (8, first.shape[1]))


def tap_weights(signal, halo, block):
    breadth, height = signal.shape
    whole = lambda shape: pl.BlockSpec(shape, lambda i: (0,) * len(shape))
    return pl.pallas_call(
        tap_kernel,
        grid=(height // COLUMNS,),
        out_shape=[
            jax.ShapeDtypeStruct((3 * breadth, height), jnp.float32),
            jax.ShapeDtypeStruct((breadth, 128), jnp.float32),
            jax.ShapeDtypeStruct((16, height), jnp.float32),
        ],
        in_specs=[
            whole(halo.shape),
            whole(signal.shape),
            pl.BlockSpec((1, COLUMNS, height), lambda i: (0, i, 0)),
        ],
        out_specs=[
            pl.BlockSpec((3 * breadth, COLUMNS), lambda i: (0, i)),
            whole((breadth, 128)),
            pl.BlockSpec((16, COLUMNS), lambda i: (0, i)),
        ],
        scratch_shapes=[pltpu.VMEM((3 * breadth, height), jnp.bfloat16)] * 2,
        compiler_params=pltpu.CompilerParams(vmem_limit_bytes=VMEM_LIMIT),
        cost_estimate=pl.CostEstimate(flops=3_600_000_000, bytes_accessed=8_000_000, transcendentals=0),
        name="tap_weights",
    )(halo, signal, block)


def send_kernel(tile_ref, weight_ref, ends_ref, edge_ref, small_in_ref, send_ref):
    breadth = ends_ref.shape[0]
    totals = [[] for _ in range(5)]
    for group in range(24):
        sums = [None] * 5
        for chunk in range(8):
            owner, tile = owner_and_tile(group, chunk)
            values = tile_ref[owner, tile]
            lanes = slice(128 * chunk, 128 * chunk + 128)
            others = [
                weight_ref[breadth * j + 8 * group : breadth * j + 8 * group + 8, lanes] for j in range(3)
            ] + [edge_ref[0:8, lanes], edge_ref[8:16, lanes]]
            for j, other in enumerate(others):
                product = values * other
                sums[j] = product if sums[j] is None else sums[j] + product
        for j in range(5):
            totals[j].append(sums[j])
    lanes = lax.broadcasted_iota(jnp.int32, (breadth, 128), 1)
    small = small_in_ref[...]
    for j in range(5):
        total = jnp.sum(jnp.concatenate(totals[j], axis=0), axis=1, keepdims=True)
        if j >= 3:
            total = total * ends_ref[:, j - 3 : j - 2]
        small = small + jnp.where(lanes == 5 + j, total, 0.0)
    rows = small.T
    tail = jnp.concatenate([rows[0:5, 128:192], rows[5:10, 128:192]], axis=1)
    packed = jnp.concatenate([rows[0:10, 0:128], tail, jnp.zeros((1, 128), jnp.float32)], axis=0)
    for block in range(BLOCKS):
        send_ref[block] = packed


def make_send(tiles, weights, ends, edges, small):
    return pl.pallas_call(
        send_kernel,
        out_shape=jax.ShapeDtypeStruct((BLOCKS, 16, 128), jnp.float32),
        in_specs=[pl.BlockSpec()] * 5,
        out_specs=pl.BlockSpec(),
        compiler_params=pltpu.CompilerParams(vmem_limit_bytes=VMEM_LIMIT),
        cost_estimate=pl.CostEstimate(flops=2_000_000, bytes_accessed=4_000_000, transcendentals=0),
        name="make_send",
    )(tiles, weights, ends, edges, small)


def inside_kernel(
    halo_ref, column_ref, tile_hbm, block_hbm, signal_hbm, query_hbm,
    out_hbm, self_ref, partner_ref,
    tile_ref, block_ref, signal_ref, query_ref, level_ref, gated_ref, sem,
):
    get_tiles = pltpu.make_async_copy(tile_hbm, tile_ref, sem.at[0])
    get_signal = pltpu.make_async_copy(signal_hbm, signal_ref, sem.at[1])
    get_query = pltpu.make_async_copy(query_hbm, query_ref, sem.at[2])
    get_block = strips(block_hbm.at[0], block_ref, sem, 3, 1)
    get_tiles.start()
    for copy in get_block:
        copy.start()
    get_signal.start()
    get_query.start()
    get_tiles.wait()
    unpack(tile_ref, level_ref, 0)
    left = split_two(level_ref[...])
    for at in range(4):
        part = slice(256 * at, 256 * at + 256)
        get_block[at].wait()
        gated_ref[:, part] = dot_three(left, split_two(block_ref[:, part]), 1, 0)
    get_signal.wait()
    get_query.wait()
    values, gated = signal_ref[...], gated_ref[...]
    prev, later = shifted(values, halo_ref[:, 0:1], halo_ref[:, 1:2])
    total = gated * conv(column_ref, 3, prev, values, later)
    rows = gated * values
    behind, ahead = shifted(rows, 0.0, 0.0)
    total = total + query_ref[...] + conv(column_ref, 3, ahead, rows, behind)
    level_ref[...] = total
    put = pltpu.make_async_copy(level_ref, out_hbm, sem.at[7])
    put.start()
    mix_ref = tile_ref.at[:, WEIGHT_TILE]
    mixes = []
    for group in range(16):
        mixes.append(mix_ref[2 * group] + mix_ref[2 * group + 1])
    for group in range(8):
        four = mix_ref[4 * group] + mix_ref[4 * group + 1] + mix_ref[4 * group + 2] + mix_ref[4 * group + 3]
        mixes.append(pltpu.roll(four, 64, 1))
    mixes = (jnp.concatenate(mixes, axis=0) * ROW_SCALE).T
    for section in range(SECTIONS):
        self_ref[section] = mixes[section : section + 1]
        partner_ref[section] = mixes[SECTIONS + section : SECTIONS + section + 1]
    put.wait()


def make_inside(tiles, block, signal, grad_query, halo, columns):
    mix = jax.ShapeDtypeStruct((SECTIONS, 1, signal.shape[0]), jnp.float32)
    buffer = pltpu.VMEM(signal.shape, jnp.float32)
    return pl.pallas_call(
        inside_kernel,
        out_shape=[jax.ShapeDtypeStruct(signal.shape, jnp.float32), mix, mix],
        in_specs=[pl.BlockSpec()] * 2 + [IN_HBM] * 4,
        out_specs=[IN_HBM] + [pl.BlockSpec()] * 2,
        scratch_shapes=[
            pltpu.VMEM(tiles.shape, jnp.float32),
            pltpu.VMEM(block.shape[1:], jnp.float32),
            buffer,
            buffer,
            buffer,
            buffer,
            pltpu.SemaphoreType.DMA((8,)),
        ],
        compiler_params=pltpu.CompilerParams(vmem_limit_bytes=VMEM_LIMIT),
        cost_estimate=pl.CostEstimate(flops=1_200_000_000, bytes_accessed=8_000_000, transcendentals=0),
        name="make_inside",
    )(halo, columns, tiles, block, signal, grad_query)


def edge_kernel(block_ref, got_ref, column_ref, in_ref, out_ref, tap_q_ref, tap_k_ref):
    at = pl.program_id(0)
    block = block_ref[0]

    def table(packed):
        low = packed[0:10]
        high = jnp.concatenate([packed[10:15, 0:64], packed[10:15, 64:128]], axis=0)
        return jnp.concatenate([low, high], axis=1)

    def columns(packed):
        rows = table(packed)
        return jnp.concatenate([rows, jnp.zeros((118, 192), jnp.float32)], axis=0).T

    source = jnp.where(at == 0, jnp.maximum(block - 1, 0), jnp.minimum(block + 1, BLOCKS - 1))
    inside = jnp.where(at == 0, block > 0, block < BLOCKS - 1)
    halo = jnp.where(inside, columns(got_ref[source]), 0.0)
    lanes = lax.broadcasted_iota(jnp.int32, (192, 128), 1)

    @pl.when(at == 0)
    def _():
        extra = column_ref[:, 2:3] * halo[:, 4:5] + column_ref[:, 5:6] * halo[:, 9:10]
        out_ref[...] = in_ref[...] + jnp.where(lanes == 0, extra, 0.0)
        sums = table(jnp.sum(got_ref[...], axis=0)) * TOKEN_SCALE
        tap_q_ref[...] = sums[0:3]
        tap_k_ref[...] = sums[5:8]

    @pl.when(at == 1)
    def _():
        extra = column_ref[:, 0:1] * halo[:, 3:4] + column_ref[:, 3:4] * halo[:, 8:9]
        out_ref[...] = in_ref[...] + jnp.where(lanes == 127, extra, 0.0)


def make_edges(block, got, columns, inside):
    whole = lambda shape: pl.BlockSpec(shape, lambda i: (0,) * len(shape))
    last = inside.shape[1] // 128 - 1
    strip = pl.BlockSpec((inside.shape[0], 128), lambda i: (0, last * i))
    return pl.pallas_call(
        edge_kernel,
        grid=(2,),
        out_shape=[
            jax.ShapeDtypeStruct(inside.shape, jnp.float32),
            jax.ShapeDtypeStruct((3, inside.shape[0]), jnp.float32),
            jax.ShapeDtypeStruct((3, inside.shape[0]), jnp.float32),
        ],
        in_specs=[
            pl.BlockSpec(memory_space=pltpu.SMEM),
            whole(got.shape),
            whole(columns.shape),
            strip,
        ],
        out_specs=[strip] + [whole((3, inside.shape[0]))] * 2,
        input_output_aliases={3: 0},
        compiler_params=pltpu.CompilerParams(vmem_limit_bytes=VMEM_LIMIT),
        cost_estimate=pl.CostEstimate(flops=200_000, bytes_accessed=900_000, transcendentals=0),
        name="make_edges",
    )(block, got, columns, inside)


def local(signal, cotangent, kernel_q, kernel_k, block_first, block_second, mix_self, mix_partner):
    before, after = neighbours(signal[-1:], signal[:1])
    signal, cotangent = signal.T, cotangent.T
    swap = lambda tiles: lax.all_to_all(tiles, "seq", 0, 0, tiled=True)
    after_both = lax.optimization_barrier
    place = lax.axis_index("ch").reshape(1)
    block = lax.axis_index("seq").reshape(1)

    packed, gated_in, grad_mixed, halo, columns = prologue(
        signal, cotangent, before, after, kernel_q, kernel_k, mix_self, mix_partner,
        block_first, block_second,
    )
    incoming = swap(packed)
    gated_other, mixed_other = other_core(gated_in), other_core(grad_mixed)
    level_last = swap(butterfly_forward(incoming))
    grad_tiles = butterfly_backward(incoming)
    tap_parts = tap_weights(signal, halo, block_first)
    level_last, grad_tiles, tap_parts, gated_other, mixed_other = after_both(
        (level_last, grad_tiles, tap_parts, gated_other, mixed_other)
    )
    returned = swap(grad_tiles)

    level_other = other_core(level_last)
    pieces = block_products(
        second_kernel, (384, 1024), "block_second_products", place,
        grad_mixed, mixed_other, level_last, level_other,
    )
    level_last, pieces = after_both((level_last, pieces))
    output, grad_query, small = make_output(
        level_last, block_second, cotangent, signal, columns, halo
    )
    second_received = receive_pieces(pieces)
    second_own = pieces[0]
    returned, small, second_received[1:] = after_both((returned, small, second_received[1:]))

    returned_other = other_core(returned)
    send = make_send(returned, *tap_parts, small)
    returned_other, send = after_both((returned_other, send))
    pieces = first_products(place, returned, returned_other, gated_in, gated_other)
    first_received = receive_pieces(pieces)
    send, pieces = after_both((send, pieces))
    got = swap(send)
    inside, mix_self_grad, mix_partner_grad = make_inside(
        returned, block_first, signal, grad_query, halo, columns
    )
    grad_second = second_own + second_received[0] + second_received[1] + second_received[2]
    grad_signal, tap_q_grad, tap_k_grad = make_edges(block, got, columns, inside)
    grad_first = pieces[0] + first_received[0] + first_received[1] + first_received[2]

    return (
        output.T,
        grad_signal.T,
        tap_q_grad,
        tap_k_grad,
        grad_first[None],
        grad_second[None],
        mix_self_grad,
        mix_partner_grad,
    )


def solution(mesh):
    return jax.shard_map(
        local,
        mesh=mesh,
        in_specs=(
            P("seq", "ch"),
            P("seq", "ch"),
            P(None, "ch"),
            P(None, "ch"),
            P("seq", None, None),
            P("seq", None, None),
            P(None, "seq", "ch"),
            P(None, "seq", "ch"),
        ),
        out_specs=(
            P("seq", "ch"),
            P("seq", "ch"),
            P(None, "ch"),
            P(None, "ch"),
            P("seq", "ch", None),
            P("seq", "ch", None),
            P(None, "seq", "ch"),
            P(None, "seq", "ch"),
        ),
        check_vma=False,
    )
```
